512 devices in a mesh: gx: 128 (over z, y_hi, x, core), gy: 4 (over y_lo).
Axes of the slice: x: 4, y: 8 (y_hi: 2, y_lo: 4; y = y_hi * 4 + y_lo), z: 8, core: 2. Of those that a mesh axis runs over, the one named last changes fastest.
Arguments:
- sensitivity: float32 [7, 2048, 128, 128], P(None, 'gx', 'gy'), may hold values from -6 to 6
- velocity: float32 [3, 2048, 128, 128], P(None, 'gx', 'gy'), may hold values from -0.1 to 0.1
- omega: float32 [2048, 128, 128], P('gx', 'gy'), may hold values from 0.8 to 1.8
- solid: int32 [2048, 128, 128], P('gx', 'gy'), may hold values 0 or 1
- active: int32 [128, 8, 8], P('gx', 'gy'), may hold values 0 or 1
Outputs:
- adjoint: float32 [7, 2048, 128, 128], P(None, 'gx', 'gy')
The draws below stay inside these ranges and needn't reach their ends.
All inputs are finite; a program needn't handle non-finite values. No bound on the sum of `solid` or of `active` on one device may be relied on, other than what follows from the above.
Results may differ from the reference program's by a relative error of at most 0.00002.
Values sent between devices are 32-bit elements; how exact they have to be, the bound alone decides.
No kernel may reach another device: no remote copies, remote signals or barrier semaphores. Data moves between devices by JAX's collectives and lax.ppermute only.
A program may use at most 64 MiB of HBM per device.

```python
import math
import jax
import jax.numpy as jnp

BLOCK = 16
ITERS = 4
NZ = 128
NX = 2048
NY = 128


def place_ends(drawn, stream_key, smallest, top_value):
    longest = drawn.shape.index(max(drawn.shape))
    spots = []
    for shift in (0, 1):
        where = [jax.random.randint(jax.random.fold_in(stream_key, axis), (), 0, length) for axis, length in enumerate(drawn.shape)]
        where[longest] = (where[longest] + shift) % drawn.shape[longest]
        spots.append(tuple(where))
    return drawn.at[spots[0]].set(smallest).at[spots[1]].set(top_value)


def level_of(own_key, extent, split, low, top_value):
    def one(position, parts):
        steps = jax.random.uniform(jax.random.fold_in(jax.random.fold_in(own_key, 6), position), (parts,), jnp.float32, low / len(split), top_value / len(split))
        return jnp.repeat(jnp.exp(steps), extent[position] // parts).reshape((-1,) + (1,) * (len(extent) - position - 1))

    level = one(*split[0])
    for cut in split[1:]:
        level = level * one(*cut)
    return level


def gaussian(rng, dims, scale, limit, pieces=(), held_as=jnp.bfloat16):
    values = scale * jax.random.normal(rng, dims, jnp.float32)
    if pieces:
        values = values * level_of(rng, dims, pieces, -0.22, 0.18)
    return jnp.clip(values, -limit, limit).astype(held_as)


def setup_inputs(seed: int = 0) -> dict:
    streams_of = jax.random.split(jax.random.key(seed), 6)
    return {
        "sensitivity": gaussian(streams_of[0], (7, NX, NY, NZ), 1.0, 6.0, ((1, 128), (2, 4)), jnp.float32),
        "velocity": jnp.clip(jax.random.uniform(streams_of[1], (3, NX, NY, NZ), jnp.float32, -0.1, 0.1) * level_of(streams_of[1], (3, NX, NY, NZ), ((1, 128), (2, 4)), -0.4, 0.0), -0.1, 0.1),
        "omega": jnp.clip(jnp.exp(math.log(1.8) - 0.8109302 * jax.random.uniform(streams_of[2], (NX, NY, NZ), jnp.float32) ** level_of(streams_of[2], (NX, NY, NZ), ((0, 128), (1, 4)), -0.2, 0.2)), 0.8, 1.8),
        "solid": place_ends((jax.random.randint(streams_of[3], (NX, NY, NZ), 0, 8) < 1).astype(jnp.int32), jax.random.fold_in(streams_of[3], 1), 0, 1),
        "active": place_ends((jax.random.randint(streams_of[4], (NX // BLOCK, NY // BLOCK, NZ // BLOCK), 0, 4) < 3).astype(jnp.int32), jax.random.fold_in(streams_of[4], 1), 0, 1),
    }


moves = ((0, 0, 0), (1, 0, 0), (-1, 0, 0), (0, 1, 0), (0, -1, 0), (0, 0, 1), (0, 0, -1))
opposite = (0, 2, 1, 4, 3, 6, 5)
weights = (0.25, 0.125, 0.125, 0.125, 0.125, 0.125, 0.125)


def adjoint_core(g_ext, stat_ext):
    width_a = g_ext.shape[1] - 2
    width_b = g_ext.shape[2] - 2
    depth_z = g_ext.shape[3]
    padded = jnp.pad(g_ext, ((0, 0), (0, 0), (0, 0), (1, 1)))
    flags = jnp.pad(stat_ext[0], ((0, 0), (0, 0), (1, 1)))
    centre = padded[:, 1:-1, 1:-1, 1:-1]
    fluid = flags[1:-1, 1:-1, 1:-1]
    inner = stat_ext[:, 1:-1, 1:-1, :]
    speed_x, speed_y, speed_z, rate = inner[1], inner[2], inner[3], inner[4]
    pulled = []
    total = jnp.zeros_like(fluid)
    for index in range(7):
        step_x, step_y, step_z = moves[index]
        near = padded[index, 1 + step_x:1 + step_x + width_a, 1 + step_y:1 + step_y + width_b, 1 + step_z:1 + step_z + depth_z]
        near_flag = flags[1 + step_x:1 + step_x + width_a, 1 + step_y:1 + step_y + width_b, 1 + step_z:1 + step_z + depth_z]
        pulled_one = near_flag * near + (1.0 - near_flag) * centre[opposite[index]]
        weight = weights[index] * (1.0 + 4.0 * (step_x * speed_x + step_y * speed_y + step_z * speed_z))
        total = total + weight * pulled_one
        pulled.append(pulled_one)
    result = [fluid * ((1.0 - rate) * pulled[index] + rate * total) for index in range(7)]
    return jnp.stack(result)


def build_static(velocity, omega, solid, active):
    expanded = jnp.repeat(jnp.repeat(jnp.repeat(active, BLOCK, axis=0), BLOCK, axis=1), BLOCK, axis=2)
    fluid = (1 - solid).astype(jnp.float32) * expanded.astype(jnp.float32)
    return jnp.stack([fluid, velocity[0], velocity[1], velocity[2], omega])


def reference(sensitivity, velocity, omega, solid, active):
    static = build_static(velocity, omega, solid, active)
    static_ext = jnp.pad(static, ((0, 0), (1, 1), (1, 1), (0, 0)))
    field = sensitivity
    for step in range(ITERS):
        field = adjoint_core(jnp.pad(field, ((0, 0), (1, 1), (1, 1), (0, 0))), static_ext)
    return field
```

```python
import jax
import jax.numpy as jnp
from jax import lax
from jax.experimental import pallas as pl
from jax.experimental.pallas import tpu as pltpu
from jax.sharding import PartitionSpec as P

BLOCK = 16
ITERS = 4
HALO = ITERS
FIELDS = 11
PARTS = 9
F32 = jnp.float32
MIB = 1 << 20

VM = pl.BlockSpec(memory_space=pltpu.VMEM)
HBM = pl.BlockSpec(memory_space=pl.ANY)
SM = pl.BlockSpec(memory_space=pltpu.SMEM)


def params(mib):
    return pltpu.CompilerParams(vmem_limit_bytes=mib * MIB)


def lane_blocks(active, row, shape):
    lane = lax.broadcasted_iota(jnp.int32, shape, 1) // BLOCK
    out = jnp.zeros(shape, jnp.int32)
    for k in range(active.shape[2]):
        out = jnp.where(lane == k, active[0, row, k], out)
    return out


def rolled(v, step, axis):
    n = v.shape[axis]
    return pltpu.roll(v, (n - step) % n, axis)


def shift_z(v, step, fill):
    lane = lax.broadcasted_iota(jnp.int32, v.shape, 1)
    edge = v.shape[1] - 1 if step > 0 else 0
    return jnp.where(lane == edge, fill, rolled(v, step, 1))


def collide(h, hu, a, bc):
    s = 0.25 * h[0] + 0.125 * ((h[1] + h[2]) + (h[3] + h[4]) + (h[5] + h[6]))
    s = s + hu[0] * (h[1] - h[2]) + hu[1] * (h[3] - h[4]) + hu[2] * (h[5] - h[6])
    t = a * s
    return [t + bc * one for one in h]


def pulled_yz(g, nyp, nym, nzp, nzm):
    return [
        rolled(g[3], 1, 0) + nyp * g[4],
        rolled(g[4], -1, 0) + nym * g[3],
        shift_z(g[5], 1, 0.0) + nzp * g[6],
        shift_z(g[6], -1, 0.0) + nzm * g[5],
    ]


def solid_flags(a):
    nf = jnp.where(a > 0.0, 0.0, 1.0).astype(F32)
    return nf, rolled(nf, 1, 0), rolled(nf, -1, 0), shift_z(nf, 1, 1.0), shift_z(nf, -1, 1.0), (1.0 - nf) - a


def pack_y(even, active, g, vel, omega, solid, msg_c, msg_d, gb, vb, ob, sb, sem):
    is_even = even[0] == 1
    ny = omega.shape[1]
    copies = []
    for side in range(2):
        row = (ny - 8) * side
        for n, (src, dst) in enumerate(((g, gb), (vel, vb), (omega, ob), (solid, sb))):
            window = src.at[:, :, pl.ds(row, 8), :] if len(src.shape) == 4 else src.at[:, pl.ds(row, 8), :]
            copies.append(pltpu.make_async_copy(window, dst.at[side], sem.at[side, n]))
    for copy in copies:
        copy.start()
    acts = [lane_blocks(active, (active.shape[1] - 1) * side, (8, 128)) for side in range(2)]
    for copy in copies:
        copy.wait()

    def plane(x, _):
        out = []
        for side in range(2):
            rows = slice(4, 8) if side else slice(0, 4)
            f = ((1 - sb[side, x]) * acts[side]).astype(F32)
            vals = [gb[side, c, x] * f for c in range(7)] + [0.5 * vb[side, c, x] for c in range(3)] + [f * ob[side, x]]
            out.append([v[rows] for v in vals])
        for c in range(FIELDS):
            low, high = out[0][c], out[1][c]
            msg_c[c, x] = jnp.where(is_even, high, low)
            msg_d[c, x] = jnp.where(is_even, low, high)
        return 0

    lax.fori_loop(0, omega.shape[0], plane, 0)


def gather_plane(x, is_even, acts, gb, vb, ob, sb, rc, rd, put):
    ny = ob.shape[1]
    half = ny // len(acts)
    f = jnp.concatenate([((1 - sb[x, n * half:(n + 1) * half]) * act).astype(F32) for n, act in enumerate(acts)], axis=0)
    for c in range(FIELDS):
        own = gb[c, x] * f if c < 7 else 0.5 * vb[c - 7, x] if c < 10 else f * ob[x]
        one, two = rc[c, x], rd[c, x]
        put(c, slice(0, HALO), jnp.where(is_even, two, one))
        put(c, slice(HALO, HALO + ny), own)
        put(c, slice(HALO + ny, 2 * HALO + ny), jnp.where(is_even, one, two))


def all_acts(active, ny):
    nb = active.shape[1]
    return [lane_blocks(active, n, (ny // nb, 128)) for n in range(nb)]


def faces(even, active, g, vel, omega, solid, rc, rd, msg_a, msg_b, st, gb, vb, ob, sb, work, sem):
    y_even, is_even = even[0] == 1, even[1] == 1
    nx, ny = omega.shape[0], omega.shape[1]
    copies = []
    for side in range(2):
        first = (nx - 4) * side
        for n, (src, dst) in enumerate(((g, gb), (vel, vb), (omega, ob), (solid, sb))):
            window = src.at[:, pl.ds(first, 4)] if len(src.shape) == 4 else src.at[pl.ds(first, 4)]
            into = dst.at[:, pl.ds(4 * side, 4)] if len(src.shape) == 4 else dst.at[pl.ds(4 * side, 4)]
            copies.append(pltpu.make_async_copy(window, into, sem.at[side, n]))
    for copy in copies:
        copy.start()
    acts = all_acts(active, ny)
    for copy in copies:
        copy.wait()

    for which in range(2):
        msg = (msg_a, msg_b)[which]
        right = is_even if which == 0 else jnp.logical_not(is_even)
        sign = jnp.where(right, 1.0, -1.0).astype(F32)
        for p in range(4):
            local = jnp.where(right, 7 - p, p)
            halo = jnp.where(right, nx - 1 - p, p)
            half = ny // len(acts)
            f = jnp.concatenate([((1 - sb[local, n * half:(n + 1) * half]) * act).astype(F32) for n, act in enumerate(acts)], axis=0)
            for c in range(FIELDS):
                real = c if c not in (1, 2) else jnp.where(right, c, 3 - c)
                own = gb[real, local] * f if c < 7 else 0.5 * vb[c - 7, local] if c < 10 else f * ob[local]
                one, two = rc[real, halo], rd[real, halo]
                low, high = jnp.where(y_even, two, one), jnp.where(y_even, one, two)
                if c == 7:
                    own, low, high = own * sign, low * sign, high * sign
                to = work.at[0, c, p] if c < 7 else st.at[which, c - 7, p]
                to[0:HALO] = low
                to[HALO:HALO + ny] = own
                to[HALO + ny:2 * HALO + ny] = high
        msg[0] = work[0, 2, 0]
        for c in range(4):
            plane = st[which, c, 0]
            msg[4 + c] = plane * sign if c == 0 else plane
        msg[8] = st[which, 3, 1] * (0.125 + st[which, 0, 1])
        flags = [solid_flags(st[which, 3, p]) for p in range(4)]
        for t in range(1, 4):
            old, new = (t - 1) % 2, t % 2
            for p in range(4 - t):
                gs = [work[old, c, p] for c in range(7)]
                nf, nyp, nym, nzp, nzm, bc = flags[p]
                if p == 0:
                    h1 = jnp.zeros_like(gs[0])
                else:
                    h1 = work[old, 1, p - 1] + flags[p - 1][0] * gs[2]
                h2 = work[old, 2, p + 1] + flags[p + 1][0] * gs[1]
                h = [gs[0], h1, h2] + pulled_yz(gs, nyp, nym, nzp, nzm)
                out = collide(h, [st[which, c, p] for c in range(3)], st[which, 3, p], bc)
                if t == 3:
                    msg[t] = out[2]
                else:
                    for c in range(7):
                        work[new, c, p] = out[c]
                    if p == 0:
                        msg[t] = out[2]


def interior(even, active, g, vel, omega, solid, rc, rd, out, ping, pong, stat, nfs):
    is_even = even[0] == 1
    nx, ny = omega.shape[0], omega.shape[1]
    acts = all_acts(active, ny)
    for buf in (ping, pong):
        for c in (1, 2):
            for x in (0, nx + 1):
                buf[c, x] = jnp.zeros(buf.shape[2:], F32)
    for x in (0, nx + 1):
        nfs[x] = jnp.zeros(nfs.shape[1:], F32)

    def build(x, _):
        def put(c, rows, value):
            if c < 7:
                ping[c, x + 1, rows] = value
            else:
                stat[c - 7, x, rows] = value

        gather_plane(x, is_even, acts, g, vel, omega, solid, rc, rd, put)
        nf, nyp, nym, nzp, nzm, bc = solid_flags(stat[3, x])
        nfs[x + 1] = nf
        for n, v in enumerate((bc, nyp, nym, nzp, nzm)):
            stat[4 + n, x] = v
        return 0

    lax.fori_loop(0, nx, build, 0)
    for t in range(ITERS):
        old, new = (ping, pong) if t % 2 == 0 else (pong, ping)

        def plane(x, _):
            gs = [old[c, x + 1] for c in range(7)]
            h1 = old[1, x + 2] + nfs[x + 2] * gs[2]
            h2 = old[2, x] + nfs[x] * gs[1]
            h = [gs[0], h1, h2] + pulled_yz(gs, stat[5, x], stat[6, x], stat[7, x], stat[8, x])
            res = collide(h, [stat[c, x] for c in range(3)], stat[3, x], stat[4, x])
            for c in range(7):
                if t == ITERS - 1:
                    out[c, x] = res[c][HALO:HALO + ny]
                else:
                    new[c, x + 1] = res[c]
            return 0

        lax.fori_loop(0, nx, plane, 0)


def respond(even, msg_a, msg_b, rec_a, rec_b, st, base, out, near, work, sem):
    is_even = even[0] == 1
    nx, ny = base.shape[1], base.shape[2]
    loads = [pltpu.make_async_copy(base.at[:, pl.ds((nx - 4) * s, 4)], near.at[:, pl.ds(4 * s, 4)], sem.at[s]) for s in range(2)]
    stores = [pltpu.make_async_copy(near.at[:, pl.ds(4 * s, 4)], out.at[:, pl.ds((nx - 4) * s, 4)], sem.at[s]) for s in range(2)]
    for copy in loads:
        copy.start()
    for copy in loads:
        copy.wait()
    for which in range(2):
        mine, theirs = ((msg_a, rec_a), (msg_b, rec_b))[which]
        right = is_even if which == 0 else jnp.logical_not(is_even)
        sign = jnp.where(right, 1.0, -1.0).astype(F32)
        hu = {1: [theirs[4] * sign, theirs[5], theirs[6]]}
        a = {1: theirs[7]}
        for p in range(4):
            hu[2 + p] = [st[which, c, p] for c in range(3)]
            a[2 + p] = st[which, 3, p]
        flags = {q: solid_flags(a[q]) for q in range(1, 6)}
        nf = {q: flags[q][0] for q in range(1, 6)}
        nf[0] = jnp.where(theirs[8] > 0.0, 0.0, 1.0).astype(F32)
        live = set()
        for t in range(ITERS):
            old, new = t % 2, (t + 1) % 2
            source = {2: theirs[t] + nf[1] * mine[t], 1: mine[t] + nf[2] * theirs[t]}

            def comp(q, c):
                return work[old, c, q] if q in live else None

            todo = ((1, 2), (0, 1, 2, 3), (1, 2, 3, 4), (2, 3, 4, 5))[t]
            for q in todo:
                if q == 0:
                    work[new, 1, 0] = theirs[8] * work[old, 2, 1]
                    continue
                gs = [comp(q, c) for c in range(7)]
                zero = jnp.zeros_like(a[q])
                here = q in live
                if here:
                    h = [gs[0], nf[q - 1] * gs[2], nf[q + 1] * gs[1] if q < 5 else zero] + pulled_yz(gs, *flags[q][1:5])
                else:
                    h = [zero] * 7
                if q - 1 in live:
                    h[1] = h[1] + work[old, 1, q - 1]
                if q + 1 in live and q >= 1:
                    h[2] = h[2] + work[old, 2, q + 1]
                if q == 2:
                    h[1] = h[1] + source[2]
                if q == 1:
                    h[2] = h[2] + source[1]
                res = collide(h, hu[q], a[q], flags[q][5])
                if t == ITERS - 1:
                    p = q - 2
                    local = jnp.where(right, 7 - p, p)
                    for c in range(7):
                        real = c if c not in (1, 2) else jnp.where(right, c, 3 - c)
                        near[real, local] = near[real, local] + res[c][HALO:HALO + ny]
                else:
                    for c in range(7):
                        work[new, c, q] = res[c]
            live = set(todo)
    for copy in stores:
        copy.start()
    for copy in stores:
        copy.wait()


def pair_up(x, axis, first):
    pairs = []
    for i in range(first, lax.axis_size(axis) - 1, 2):
        pairs += [(i, i + 1), (i + 1, i)]
    return lax.ppermute(x, axis, pairs)


def call(kernel, outs, ins, out_specs, scratch, mib, cost, **more):
    return pl.pallas_call(
        kernel,
        out_shape=outs,
        in_specs=ins,
        out_specs=out_specs,
        scratch_shapes=scratch,
        compiler_params=params(mib),
        cost_estimate=pl.CostEstimate(flops=cost, bytes_accessed=8 * MIB, transcendentals=0),
        **more,
    )


def on_device(sensitivity, velocity, omega, solid, active):
    nx, ny, nz = omega.shape
    rows = ny + 2 * HALO
    f32 = lambda *shape: jax.ShapeDtypeStruct(shape, F32)
    even_x = (1 - lax.axis_index("gx") % 2).astype(jnp.int32)[None]
    even_y = (1 - lax.axis_index("gy") % 2).astype(jnp.int32)[None]
    vm = pltpu.VMEM
    dma = pltpu.SemaphoreType.DMA

    msg_c, msg_d = call(
        pack_y,
        (f32(FIELDS, nx, HALO, nz),) * 2,
        [SM, SM, HBM, HBM, HBM, HBM],
        (VM, VM),
        [vm((2, 7, nx, 8, nz), F32), vm((2, 3, nx, 8, nz), F32), vm((2, nx, 8, nz), F32), vm((2, nx, 8, nz), jnp.int32), dma((2, 4))],
        24,
        1 << 20,
    )(even_y, active, sensitivity, velocity, omega, solid)
    rec_c = pair_up(msg_c, "gy", 0)
    rec_d = pair_up(msg_d, "gy", 1)

    even = jnp.concatenate([even_y, even_x])
    msg_a, msg_b, st = call(
        faces,
        (f32(PARTS, rows, nz),) * 2 + (f32(2, 4, 4, rows, nz),),
        [SM, SM, HBM, HBM, HBM, HBM, VM, VM],
        (VM, VM, VM),
        [vm((7, 8, ny, nz), F32), vm((3, 8, ny, nz), F32), vm((8, ny, nz), F32), vm((8, ny, nz), jnp.int32), vm((2, 7, 4, rows, nz), F32), dma((2, 4))],
        24,
        1 << 20,
    )(even, active, sensitivity, velocity, omega, solid, rec_c, rec_d)
    rec_a = pair_up(msg_a, "gx", 0)
    rec_b = pair_up(msg_b, "gx", 1)

    base = call(
        interior,
        f32(7, nx, ny, nz),
        [SM, SM, VM, VM, VM, VM, VM, VM],
        VM,
        [vm((7, nx + 2, rows, nz), F32), vm((7, nx + 2, rows, nz), F32), vm((9, nx, rows, nz), F32), vm((nx + 2, rows, nz), F32)],
        32,
        1 << 24,
    )(even_y, active, sensitivity, velocity, omega, solid, rec_c, rec_d)

    return call(
        respond,
        f32(7, nx, ny, nz),
        [SM, VM, VM, VM, VM, VM, HBM],
        HBM,
        [vm((7, 8, ny, nz), F32), vm((2, 7, 6, rows, nz), F32), dma((2,))],
        24,
        1 << 20,
        input_output_aliases={6: 0},
    )(even_x, msg_a, msg_b, rec_a, rec_b, st, base)


def solution(mesh):
    in_specs = (
        P(None, "gx", "gy", None),
        P(None, "gx", "gy", None),
        P("gx", "gy", None),
        P("gx", "gy", None),
        P("gx", "gy", None),
    )
    out_specs = P(None, "gx", "gy", None)
    return jax.shard_map(
        on_device, mesh=mesh, in_specs=in_specs, out_specs=out_specs, check_vma=False
    )
```

```python
import functools

import jax
import jax.numpy as jnp
from jax import lax
from jax.experimental import pallas as pl
from jax.experimental.pallas import tpu as pltpu
from jax.sharding import PartitionSpec as P

BLOCK = 16
ITERS = 4
TILE = 8
FIELDS = 11
FLUX = FIELDS
CORNER = FIELDS + 4
ROWS = CORNER + 2
PARTS = 9
F32 = jnp.float32
MIB = 1 << 20

VM = pl.BlockSpec(memory_space=pltpu.VMEM)
HBM = pl.BlockSpec(memory_space=pl.ANY)
SM = pl.BlockSpec(memory_space=pltpu.SMEM)


def params(mib):
    return pltpu.CompilerParams(vmem_limit_bytes=mib * MIB)


def even_index(axis):
    return lax.axis_index(axis) % 2 == 0


def lane_blocks(active, row, shape):
    lane = lax.broadcasted_iota(jnp.int32, shape, 1) // BLOCK
    out = jnp.zeros(shape, jnp.int32)
    for k in range(active.shape[2]):
        out = jnp.where(lane == k, active[0, row, k], out)
    return out


def rolled(v, step, axis):
    n = v.shape[axis]
    return pltpu.roll(v, (n - step) % n, axis)


def shift_z(v, step, fill):
    lane = lax.broadcasted_iota(jnp.int32, v.shape, 1)
    edge = v.shape[1] - 1 if step > 0 else 0
    return jnp.where(lane == edge, fill, rolled(v, step, 1))


def collide(h, hu, a, bc):
    s = 0.25 * h[0] + 0.125 * ((h[1] + h[2]) + (h[3] + h[4]) + (h[5] + h[6]))
    s = s + hu[0] * (h[1] - h[2]) + hu[1] * (h[3] - h[4]) + hu[2] * (h[5] - h[6])
    t = a * s
    return [t + bc * one for one in h]


def write_flags(a_ref, flags):
    a = a_ref[...]
    nf = jnp.where(a > 0.0, 0.0, 1.0).astype(F32)
    flags[0] = rolled(nf, 1, 0)
    flags[1] = rolled(nf, -1, 0)
    flags[2] = shift_z(nf, 1, 1.0)
    flags[3] = shift_z(nf, -1, 1.0)
    flags[4] = (1.0 - nf) - a
    flags[5] = nf


def advance(tiles, g, pull_1, pull_2, hu, a, flags, put, drop=None):
    if g is not None:
        g3, g4 = g[3][...], g[4][...]
        up, down = rolled(g3, 1, 0), rolled(g4, -1, 0)
    for i in range(tiles):
        r = slice(TILE * i, TILE * i + TILE)
        if g is None:
            zero = jnp.zeros((TILE, a.shape[1]), F32)
            h = [zero, pull_1(r, zero), pull_2(r, zero), zero, zero, zero, zero]
        else:
            g1, g2, g5, g6 = (g[c][r] for c in (1, 2, 5, 6))
            h = [
                g[0][r],
                pull_1(r, g2),
                pull_2(r, g1),
                up[r] + flags[0, r] * g4[r],
                down[r] + flags[1, r] * g3[r],
                shift_z(g5, 1, 0.0) + flags[2, r] * g6,
                shift_z(g6, -1, 0.0) + flags[3, r] * g5,
            ]
        if drop is not None:
            h[drop] = jnp.zeros_like(h[drop])
        put(r, collide(h, [one[r] for one in hu], a[r], flags[4, r]), h)


def pack_rows(active, g, vel, omega, solid, msg_c, msg_d, gb, vb, ob, sb, ping, pong, stat, fl, sem):
    is_even = even_index("gy")
    nx, ny = omega.shape[0], omega.shape[1]
    copies = []
    for side in range(2):
        row = (ny - TILE) * side
        for n, (src, dst) in enumerate(((solid, sb), (omega, ob), (vel, vb), (g, gb))):
            window = src.at[:, :, pl.ds(row, TILE), :] if len(src.shape) == 4 else src.at[:, pl.ds(row, TILE), :]
            copies.append(pltpu.make_async_copy(window, dst.at[side], sem.at[side, n]))
    for copy in copies:
        copy.start()
    acts = [lane_blocks(active, (active.shape[1] - 1) * side, (TILE, 128)) for side in range(2)]
    zero = jnp.zeros((TILE, 128), F32)
    for side in range(2):
        for x in (0, nx + 1):
            fl[side, x, 5] = zero
            for c in (1, 2):
                ping[side, c, x] = zero
                pong[side, c, x] = zero
    for copy in copies:
        copy.wait()

    def send(k, x, values, row):
        low, high = values[0][row:row + 1], values[1][TILE - 1 - row:TILE - row]
        msg_c[k, x] = jnp.where(is_even, high, low)
        msg_d[k, x] = jnp.where(is_even, low, high)

    def build(x, _):
        fields = []
        for side in range(2):
            f = ((1 - sb[side, x]) * acts[side]).astype(F32)
            vals = [gb[side, c, x] * f for c in range(7)] + [0.5 * vb[side, c, x] for c in range(3)] + [f * ob[side, x]]
            for c in range(FIELDS):
                if c < 7:
                    ping[side, c, x + 1] = vals[c]
                else:
                    stat[side, c - 7, x] = vals[c]
            write_flags(stat.at[side, 3, x], fl.at[side, x + 1])
            fields.append(vals)
        for c in range(FIELDS):
            send(c, x, [fields[0][c], fields[1][c]], 0)
        send(FLUX, x, [fields[0][3], fields[1][4]], 1)
        send(FLUX + 3, x, [fields[0][10] * (0.125 - fields[0][8]), fields[1][10] * (0.125 + fields[1][8])], 1)
        return 0

    lax.fori_loop(0, nx, build, 0, unroll=16)

    def step(x, t):
        old, new = (ping, pong) if t == 0 else (pong, ping)
        fluxes = []
        for side in range(2):

            def pull_1(r, g2):
                return old[side, 1, x + 2, r] + fl[side, x + 2, 5, r] * g2

            def pull_2(r, g1):
                return old[side, 2, x, r] + fl[side, x, 5, r] * g1

            def put(r, res, h):
                if t == 0:
                    for c in range(7):
                        new[side, c, x + 1, r] = res[c]
                fluxes.append(res[3 + side])

            gs = [old.at[side, c, x + 1] for c in range(7)]
            advance(1, gs, pull_1, pull_2, [stat.at[side, c, x] for c in range(3)], stat.at[side, 3, x], fl.at[side, x + 1], put, None if t == 0 else 4 - side)
        send(FLUX + 1 + t, x, fluxes, 1)

    for t in range(2):

        def plane(x, _):
            step(x, t)
            return 0

        lax.fori_loop(0, nx, plane, 0, unroll=16)

    for face in range(2):
        at = [nx - 1 if face else 0, nx - 2 if face else 1]
        for n, (p, row) in enumerate(((0, 1), (0, 2), (1, 1))):
            for c in range(4):
                send(CORNER + face, 4 * n + c, [stat[side, c, at[p]] for side in range(2)], row)
        for n, (buf, row) in enumerate(((None, 1), (pong, 1), (None, 2))):
            if buf is None:
                f = [((1 - sb[side, at[0]]) * acts[side]).astype(F32) for side in range(2)]
                send(CORNER + face, 12 + n, [gb[side, 1 + face, at[0]] * f[side] for side in range(2)], row)
            else:
                send(CORNER + face, 12 + n, [buf[side, 1 + face, at[0] + 1] for side in range(2)], row)
        msg_c[CORNER + face, 15] = zero[:1]
        msg_d[CORNER + face, 15] = zero[:1]


def halo_rows(rc, rd, y_even):
    def row(k, x):
        one, two = rc[k, x], rd[k, x]
        return jnp.where(y_even, one, two), jnp.where(y_even, two, one)

    return row


def placed(tile, rows, at):
    sub = lax.broadcasted_iota(jnp.int32, (TILE, 128), 0)
    return jnp.where(sub == at, rows[0], jnp.where(sub == TILE - 1 - at, rows[1], tile))


def with_flux(res, h, rows, t, x):
    sub = lax.broadcasted_iota(jnp.int32, (TILE, 128), 0)
    high, low = rows(FLUX + t, x)
    if t == 2:
        k = rows(FLUX + 3, x)
        high, low = high + k[0] * h[4], low + k[1] * h[3]
    res[3] = jnp.where(sub == 1, high, res[3])
    res[4] = jnp.where(sub == TILE - 2, low, res[4])


def all_acts(active, ny):
    nb = active.shape[1]
    return [lane_blocks(active, n, (ny // nb, 128)) for n in range(nb)]


def gather_plane(x, acts, g, vel, omega, solid, halo, dest, mirror):
    ny = omega.shape[1]
    half = ny // len(acts)
    f = jnp.concatenate([((1 - solid[x, n * half:(n + 1) * half]) * act).astype(F32) for n, act in enumerate(acts)], axis=0)
    for c in range(FIELDS):
        real = c
        if mirror is not None and c in (1, 2):
            real = jnp.where(mirror[0], c, 3 - c)
        own = g[real, x] * f if c < 7 else 0.5 * vel[c - 7, x] if c < 10 else f * omega[x]
        rest = halo(real)
        if mirror is not None and c == 7:
            own, rest = own * mirror[1], rest * mirror[1]
        to = dest(c)
        to[0:ny] = own
        to[ny:ny + TILE] = rest


def face(which, active, g, vel, omega, solid, rc, rd, msg, st, work, fl):
    y_even, x_even = even_index("gy"), even_index("gx")
    nx, ny = omega.shape[0], omega.shape[1]
    tiles = work.shape[3] // TILE
    right = x_even if which == 0 else jnp.logical_not(x_even)
    sign = jnp.where(right, 1.0, -1.0).astype(F32)
    acts = all_acts(active, ny)
    rows = halo_rows(rc, rd, y_even)
    corner = jnp.where(right, CORNER + 1, CORNER)
    where = [jnp.where(right, nx - 1 - p, p) for p in range(4)]
    for p in range(4):

        def halo(c):
            tile = placed(jnp.zeros((TILE, 128), F32), rows(c, where[p]), 0)
            if isinstance(c, int) and c in (3, 4):
                high, low = rows(FLUX, where[p])
                sub = lax.broadcasted_iota(jnp.int32, (TILE, 128), 0)
                tile = jnp.where(sub == (1 if c == 3 else TILE - 2), high if c == 3 else low, tile)
            if isinstance(c, int) and c >= 7:
                if p == 0:
                    tile = placed(placed(tile, rows(corner, c - 7), 1), rows(corner, c - 3), 2)
                if p == 1:
                    tile = placed(tile, rows(corner, c + 1), 1)
            return tile

        gather_plane(where[p], acts, g, vel, omega, solid, halo, lambda c: work.at[0, c, p] if c < 7 else st.at[c - 7, p], (right, sign))
        write_flags(st.at[3, p], fl.at[p])
    last = slice(ny, ny + TILE)
    msg[0, 0:ny] = work[0, 2, 0, 0:ny]
    msg[0, last] = placed(placed(work[0, 2, 0, last], rows(corner, 12), 1), rows(corner, 14), 2)
    msg[4] = st[0, 0] * sign
    for c in range(1, 4):
        msg[4 + c] = st[c, 0]
    msg[8] = st[3, 1] * (0.125 + st[0, 1])
    for t in range(1, 4):
        old, new = (t - 1) % 2, t % 2
        for p in range(4 - t):

            def pull_1(r, g2):
                if p == 0:
                    return jnp.zeros_like(g2)
                return work[old, 1, p - 1, r] + fl[p - 1, 5, r] * g2

            def pull_2(r, g1):
                return work[old, 2, p + 1, r] + fl[p + 1, 5, r] * g1

            def put(r, out, h):
                if t == 1 and r == last:
                    with_flux(out, h, rows, t, where[p])
                if p == 0:
                    msg[t, r] = placed(out[2], rows(corner, 13), 1) if t == 1 and r == last else out[2]
                if t < 3:
                    for c in range(7):
                        work[new, c, p, r] = out[c]

            gs = [work.at[old, c, p] for c in range(7)]
            advance(tiles, gs, pull_1, pull_2, [st.at[c, p] for c in range(3)], st.at[3, p], fl.at[p], put)


def interior(active, g, vel, omega, solid, rc, rd, out, near, ping, pong, stat, fl, mid, sem):
    y_even = even_index("gy")
    nx, ny = omega.shape[0], omega.shape[1]
    tiles = ping.shape[2] // TILE
    acts = all_acts(active, ny)
    rows = halo_rows(rc, rd, y_even)
    for x in (0, nx + 1):
        for buf in (ping, pong):
            for c in (1, 2):
                buf[c, x] = jnp.zeros(buf.shape[2:], F32)
        fl[x, 5] = jnp.zeros(fl.shape[2:], F32)

    def build(x, _):
        def halo(c):
            tile = placed(jnp.zeros((TILE, 128), F32), rows(c, x), 0)
            sub = lax.broadcasted_iota(jnp.int32, (TILE, 128), 0)
            if c in (3, 4):
                high, low = rows(FLUX, x)
                tile = jnp.where(sub == (1 if c == 3 else TILE - 2), high if c == 3 else low, tile)
            if c == 10:
                tile = placed(tile, rows(FLUX + 3, x), 1)
            return tile

        gather_plane(x, acts, g, vel, omega, solid, halo, lambda c: ping.at[c, x + 1] if c < 7 else stat.at[c - 7, x], None)
        write_flags(stat.at[3, x], fl.at[x + 1])
        return 0

    lax.fori_loop(0, nx, build, 0, unroll=16)

    for t in range(ITERS):
        old, new = (ping, pong) if t % 2 == 0 else (pong, ping)

        def run(x, tiles, put):
            def pull_1(r, g2):
                return old[1, x + 2, r] + fl[x + 2, 5, r] * g2

            def pull_2(r, g1):
                return old[2, x, r] + fl[x, 5, r] * g1

            gs = [old.at[c, x + 1] for c in range(7)]
            advance(tiles, gs, pull_1, pull_2, [stat.at[c, x] for c in range(3)], stat.at[3, x], fl.at[x + 1], put)

        if t < ITERS - 1:

            def plane(x, _):
                def put(r, res, h):
                    if t < 2 and r.start == ny:
                        with_flux(res, h, rows, t + 1, x)
                    for c in range(7):
                        new[c, x + 1, r] = res[c]

                run(x, tiles, put)
                return 0

            lax.fori_loop(0, nx, plane, 0, unroll=16)
        else:

            def last(into, shift):
                def plane(x, _):
                    def put(r, res, h):
                        for c in range(7):
                            into[c, x - shift, r] = res[c]

                    run(x, ny // TILE, put)
                    return 0

                return plane

            lax.fori_loop(4, nx - 4, last(mid, 4), 0, unroll=4)
            store = pltpu.make_async_copy(mid, out.at[:, pl.ds(4, nx - 8)], sem.at[0])
            store.start()
            lax.fori_loop(0, 4, last(near, 0), 0, unroll=4)
            lax.fori_loop(nx - 4, nx, last(near, nx - 8), 0, unroll=4)
            store.wait()


def respond(msg_a, msg_b, rec_a, rec_b, st_a, st_b, near, base, out, work, fl, hu1, done, sem):
    is_even = even_index("gx")
    nx, ny = base.shape[1], base.shape[2]
    tiles = work.shape[3] // TILE
    for which in range(2):
        mine, theirs, st = ((msg_a, rec_a, st_a), (msg_b, rec_b, st_b))[which]
        right = is_even if which == 0 else jnp.logical_not(is_even)
        sign = jnp.where(right, 1.0, -1.0).astype(F32)
        hu1[...] = theirs[4] * sign
        hu = {1: [hu1, theirs.at[5], theirs.at[6]]}
        a = {1: theirs.at[7]}
        for p in range(4):
            hu[2 + p] = [st.at[c, p] for c in range(3)]
            a[2 + p] = st.at[3, p]
        for q in range(1, 6):
            write_flags(a[q], fl.at[q])
        fl[0, 5] = jnp.where(theirs[8] > 0.0, 0.0, 1.0).astype(F32)
        live = set()
        for t in range(ITERS):
            old, new = t % 2, (t + 1) % 2
            todo = ((1, 2), (0, 1, 2, 3), (1, 2, 3, 4), (2, 3, 4, 5))[t]
            for q in todo:
                if q == 0:
                    work[new, 1, 0] = theirs[8] * work[old, 2, 1]
                    continue

                def pull_1(r, g2):
                    h = fl[q - 1, 5, r] * g2 if q in live else g2
                    if q - 1 in live:
                        h = h + work[old, 1, q - 1, r]
                    if q == 2:
                        h = h + (theirs[t, r] + fl[1, 5, r] * mine[t, r])
                    return h

                def pull_2(r, g1):
                    h = fl[q + 1, 5, r] * g1 if q in live else g1
                    if q + 1 in live:
                        h = h + work[old, 2, q + 1, r]
                    if q == 1:
                        h = h + (mine[t, r] + fl[2, 5, r] * theirs[t, r])
                    return h

                def put(r, res, h):
                    if t < ITERS - 1:
                        for c in range(7):
                            work[new, c, q, r] = res[c]
                        return
                    local = jnp.where(right, 9 - q, q - 2)
                    for c in range(7):
                        real = c if c not in (1, 2) else jnp.where(right, c, 3 - c)
                        done[real, local, r] = near[real, local, r] + res[c]

                gs = [work.at[old, c, q] for c in range(7)] if q in live else None
                advance(tiles if t < ITERS - 1 else ny // TILE, gs, pull_1, pull_2, hu[q], a[q], fl.at[q], put)
            live = set(todo)
        if which == 0:
            first = jnp.where(right, 1, 0)
            store = pltpu.make_async_copy(done.at[:, pl.ds(4 * first, 4)], out.at[:, pl.ds((nx - 4) * first, 4)], sem.at[0])
            store.start()
    first = 1 - first
    other = pltpu.make_async_copy(done.at[:, pl.ds(4 * first, 4)], out.at[:, pl.ds((nx - 4) * first, 4)], sem.at[1])
    other.start()
    store.wait()
    other.wait()


def pair_up(x, axis, first):
    pairs = []
    for i in range(first, lax.axis_size(axis) - 1, 2):
        pairs += [(i, i + 1), (i + 1, i)]
    return lax.ppermute(x, axis, pairs)


def call(kernel, outs, ins, out_specs, scratch, mib, cost, **more):
    return pl.pallas_call(
        kernel,
        out_shape=outs,
        in_specs=ins,
        out_specs=out_specs,
        scratch_shapes=scratch,
        compiler_params=params(mib),
        cost_estimate=pl.CostEstimate(flops=cost, bytes_accessed=4 * MIB, transcendentals=0),
        **more,
    )


def on_device(sensitivity, velocity, omega, solid, active):
    nx, ny, nz = omega.shape
    rows = ny + TILE
    f32 = lambda *shape: jax.ShapeDtypeStruct(shape, F32)
    vm = pltpu.VMEM
    dma = pltpu.SemaphoreType.DMA

    pinned = [pltpu.with_memory_space_constraint(v, pltpu.HBM) for v in (active, sensitivity, velocity, omega, solid)]
    edge = lambda *shape: vm((2,) + shape + (TILE, nz), F32)
    msg_c, msg_d = call(
        pack_rows,
        (f32(ROWS, nx, 1, nz),) * 2,
        [SM, HBM, HBM, HBM, HBM],
        (VM,) * 2,
        [edge(7, nx), edge(3, nx), edge(nx), vm((2, nx, TILE, nz), jnp.int32), edge(7, nx + 2), edge(7, nx + 2), edge(4, nx), edge(nx + 2, 6), dma((2, 4))],
        24,
        1 << 20,
    )(*pinned)
    rec_c = pair_up(msg_c, "gy", 0)
    rec_d = pair_up(msg_d, "gy", 1)

    def message(which):
        return call(
            functools.partial(face, which),
            (f32(PARTS, rows, nz), f32(4, 4, rows, nz)),
            [SM, VM, VM, VM, VM, VM, VM],
            (VM, VM),
            [vm((2, 7, 4, rows, nz), F32), vm((4, 6, rows, nz), F32)],
            24,
            1 << 20,
        )(active, sensitivity, velocity, omega, solid, rec_c, rec_d)

    msg_b, st_b = message(1)
    rec_b = pair_up(msg_b, "gx", 1)
    msg_a, st_a = message(0)
    rec_a = pair_up(msg_a, "gx", 0)

    base, near = call(
        interior,
        (f32(7, nx, ny, nz), f32(7, 8, ny, nz)),
        [SM, VM, VM, VM, VM, VM, VM],
        (HBM, VM),
        [
            vm((7, nx + 2, rows, nz), F32),
            vm((7, nx + 2, rows, nz), F32),
            vm((4, nx, rows, nz), F32),
            vm((nx + 2, 6, rows, nz), F32),
            vm((7, nx - 8, ny, nz), F32),
            dma((1,)),
        ],
        32,
        1 << 24,
    )(active, sensitivity, velocity, omega, solid, rec_c, rec_d)

    return call(
        respond,
        f32(7, nx, ny, nz),
        [VM, VM, VM, VM, VM, VM, VM, HBM],
        HBM,
        [vm((2, 7, 6, rows, nz), F32), vm((6, 6, rows, nz), F32), vm((rows, nz), F32), vm((7, 8, ny, nz), F32), dma((2,))],
        24,
        1 << 20,
        input_output_aliases={7: 0},
    )(msg_a, msg_b, rec_a, rec_b, st_a, st_b, near, base)


def solution(mesh):
    in_specs = (
        P(None, "gx", "gy", None),
        P(None, "gx", "gy", None),
        P("gx", "gy", None),
        P("gx", "gy", None),
        P("gx", "gy", None),
    )
    out_specs = P(None, "gx", "gy", None)
    return jax.shard_map(
        on_device, mesh=mesh, in_specs=in_specs, out_specs=out_specs, check_vma=False
    )
```

```python
import functools

import jax
import jax.numpy as jnp
from jax import lax
from jax.experimental import pallas as pl
from jax.experimental.pallas import tpu as pltpu
from jax.sharding import PartitionSpec as P

BLOCK = 16
ITERS = 4
TILE = 8
FIELDS = 11
FLUX = FIELDS
CORNER = FIELDS + 4
ROWS = CORNER + 2
PARTS = 9
F32 = jnp.float32
MIB = 1 << 20

VM = pl.BlockSpec(memory_space=pltpu.VMEM)
HBM = pl.BlockSpec(memory_space=pl.ANY)


def params(mib):
    return pltpu.CompilerParams(vmem_limit_bytes=mib * MIB)


def even_index(axis):
    return lax.axis_index(axis) % 2 == 0


def lane_blocks(active, row, shape):
    lane = lax.broadcasted_iota(jnp.int32, shape, 1) // BLOCK
    out = jnp.zeros(shape, jnp.int32)
    for k in range(active.shape[1]):
        out = jnp.where(lane == k, jnp.broadcast_to(active[row:row + 1, k:k + 1], shape), out)
    return out


def rolled(v, step, axis):
    n = v.shape[axis]
    return pltpu.roll(v, (n - step) % n, axis)


def shift_z(v, step, fill):
    lane = lax.broadcasted_iota(jnp.int32, v.shape, 1)
    edge = v.shape[1] - 1 if step > 0 else 0
    return jnp.where(lane == edge, fill, rolled(v, step, 1))


def collide(h, hu, a, bc):
    s = 0.25 * h[0] + 0.125 * ((h[1] + h[2]) + (h[3] + h[4]) + (h[5] + h[6]))
    s = s + hu[0] * (h[1] - h[2]) + hu[1] * (h[3] - h[4]) + hu[2] * (h[5] - h[6])
    t = a * s
    return [t + bc * one for one in h]


def write_flags(a_ref, flags):
    a = a_ref[...]
    nf = jnp.where(a > 0.0, 0.0, 1.0).astype(F32)
    flags[0] = rolled(nf, 1, 0)
    flags[1] = rolled(nf, -1, 0)
    flags[2] = shift_z(nf, 1, 1.0)
    flags[3] = shift_z(nf, -1, 1.0)
    flags[4] = (1.0 - nf) - a
    flags[5] = nf


def advance(tiles, g, pull_1, pull_2, hu, a, flags, put, drop=None):
    if g is not None:
        g3, g4 = g[3][...], g[4][...]
        up, down = rolled(g3, 1, 0), rolled(g4, -1, 0)
    for i in range(tiles):
        r = slice(TILE * i, TILE * i + TILE)
        if g is None:
            zero = jnp.zeros((TILE, a.shape[1]), F32)
            h = [zero, pull_1(r, zero), pull_2(r, zero), zero, zero, zero, zero]
        else:
            g1, g2, g5, g6 = (g[c][r] for c in (1, 2, 5, 6))
            h = [
                g[0][r],
                pull_1(r, g2),
                pull_2(r, g1),
                up[r] + flags[0, r] * g4[r],
                down[r] + flags[1, r] * g3[r],
                shift_z(g5, 1, 0.0) + flags[2, r] * g6,
                shift_z(g6, -1, 0.0) + flags[3, r] * g5,
            ]
        if drop is not None:
            h[drop] = jnp.zeros_like(h[drop])
        put(r, collide(h, [one[r] for one in hu], a[r], flags[4, r]), h)


def pack_rows(active, g, vel, omega, solid, msg_c, msg_d, gb, vb, ob, sb, ab, ping, pong, stat, fl, sem):
    is_even = even_index("gy")
    nx, ny = omega.shape[0], omega.shape[1]
    copies = []
    for side in range(2):
        row = (ny - TILE) * side
        for n, (src, dst) in enumerate(((solid, sb), (omega, ob), (vel, vb), (g, gb))):
            window = src.at[:, :, pl.ds(row, TILE), :] if len(src.shape) == 4 else src.at[:, pl.ds(row, TILE), :]
            copies.append(pltpu.make_async_copy(window, dst.at[side], sem.at[side, n]))
    copies.append(pltpu.make_async_copy(active, ab, sem.at[2, 0]))
    for copy in reversed(copies):
        copy.start()
    zero = jnp.zeros((TILE, 128), F32)
    for side in range(2):
        for x in (0, nx + 1):
            fl[side, x, 5] = zero
            for c in (1, 2):
                ping[side, c, x] = zero
                pong[side, c, x] = zero
    copies[-1].wait()
    acts = [lane_blocks(ab[0], (active.shape[1] - 1) * side, (TILE, 128)) for side in range(2)]
    for copy in copies[:-1]:
        copy.wait()

    def send(k, x, values, row):
        low, high = values[0][row:row + 1], values[1][TILE - 1 - row:TILE - row]
        msg_c[k, x] = jnp.where(is_even, high, low)
        msg_d[k, x] = jnp.where(is_even, low, high)

    def build(x, _):
        fields = []
        for side in range(2):
            f = ((1 - sb[side, x]) * acts[side]).astype(F32)
            vals = [gb[side, c, x] * f for c in range(7)] + [0.5 * vb[side, c, x] for c in range(3)] + [f * ob[side, x]]
            for c in range(FIELDS):
                if c < 7:
                    ping[side, c, x + 1] = vals[c]
                else:
                    stat[side, c - 7, x] = vals[c]
            write_flags(stat.at[side, 3, x], fl.at[side, x + 1])
            fields.append(vals)
        for c in range(FIELDS):
            send(c, x, [fields[0][c], fields[1][c]], 0)
        send(FLUX, x, [fields[0][3], fields[1][4]], 1)
        send(FLUX + 3, x, [fields[0][10] * (0.125 - fields[0][8]), fields[1][10] * (0.125 + fields[1][8])], 1)
        return 0

    lax.fori_loop(0, nx, build, 0, unroll=16)

    def step(x, t):
        old, new = (ping, pong) if t == 0 else (pong, ping)
        fluxes = []
        for side in range(2):

            def pull_1(r, g2):
                return old[side, 1, x + 2, r] + fl[side, x + 2, 5, r] * g2

            def pull_2(r, g1):
                return old[side, 2, x, r] + fl[side, x, 5, r] * g1

            def put(r, res, h):
                if t == 0:
                    for c in range(7):
                        new[side, c, x + 1, r] = res[c]
                fluxes.append(res[3 + side])

            gs = [old.at[side, c, x + 1] for c in range(7)]
            advance(1, gs, pull_1, pull_2, [stat.at[side, c, x] for c in range(3)], stat.at[side, 3, x], fl.at[side, x + 1], put, None if t == 0 else 4 - side)
        send(FLUX + 1 + t, x, fluxes, 1)

    for t in range(2):

        def plane(x, _):
            step(x, t)
            return 0

        lax.fori_loop(0, nx, plane, 0, unroll=16)

    for face in range(2):
        at = [nx - 1 if face else 0, nx - 2 if face else 1]
        for n, (p, row) in enumerate(((0, 1), (0, 2), (1, 1))):
            for c in range(4):
                send(CORNER + face, 4 * n + c, [stat[side, c, at[p]] for side in range(2)], row)
        for n, (buf, row) in enumerate(((None, 1), (pong, 1), (None, 2))):
            if buf is None:
                f = [((1 - sb[side, at[0]]) * acts[side]).astype(F32) for side in range(2)]
                send(CORNER + face, 12 + n, [gb[side, 1 + face, at[0]] * f[side] for side in range(2)], row)
            else:
                send(CORNER + face, 12 + n, [buf[side, 1 + face, at[0] + 1] for side in range(2)], row)
        msg_c[CORNER + face, 15] = zero[:1]
        msg_d[CORNER + face, 15] = zero[:1]


def halo_rows(rc, rd, y_even):
    def row(k, x):
        one, two = rc[k, x], rd[k, x]
        return jnp.where(y_even, one, two), jnp.where(y_even, two, one)

    return row


def placed(tile, rows, at):
    sub = lax.broadcasted_iota(jnp.int32, (TILE, 128), 0)
    return jnp.where(sub == at, rows[0], jnp.where(sub == TILE - 1 - at, rows[1], tile))


def with_flux(res, h, rows, t, x):
    sub = lax.broadcasted_iota(jnp.int32, (TILE, 128), 0)
    high, low = rows(FLUX + t, x)
    if t == 2:
        k = rows(FLUX + 3, x)
        high, low = high + k[0] * h[4], low + k[1] * h[3]
    res[3] = jnp.where(sub == 1, high, res[3])
    res[4] = jnp.where(sub == TILE - 2, low, res[4])


def all_acts(active, ny):
    nb = active.shape[1]
    return [lane_blocks(active[0], n, (ny // nb, 128)) for n in range(nb)]


def gather_plane(x, acts, g, vel, omega, solid, halo, dest, mirror):
    ny = omega.shape[1]
    half = ny // len(acts)
    f = jnp.concatenate([((1 - solid[x, n * half:(n + 1) * half]) * act).astype(F32) for n, act in enumerate(acts)], axis=0)
    for c in range(FIELDS):
        real = c
        if mirror is not None and c in (1, 2):
            real = jnp.where(mirror[0], c, 3 - c)
        own = g[real, x] * f if c < 7 else 0.5 * vel[c - 7, x] if c < 10 else f * omega[x]
        rest = halo(real)
        if mirror is not None and c == 7:
            own, rest = own * mirror[1], rest * mirror[1]
        to = dest(c)
        to[0:ny] = own
        to[ny:ny + TILE] = rest


def face(which, active, g, vel, omega, solid, rc, rd, *rest):
    msg, st, fl, work = rest[-4:]
    y_even, x_even = even_index("gy"), even_index("gx")
    rc = rc.at[jnp.where(y_even, 1, 0)]
    nx, ny = omega.shape[0], omega.shape[1]
    tiles = work.shape[3] // TILE
    right = x_even if which == 0 else jnp.logical_not(x_even)
    sign = jnp.where(right, 1.0, -1.0).astype(F32)
    acts = all_acts(active, ny)
    rows = halo_rows(rc, rd, y_even)
    corner = jnp.where(right, CORNER + 1, CORNER)
    where = [jnp.where(right, nx - 1 - p, p) for p in range(4)]
    for p in range(4):

        def halo(c):
            tile = placed(jnp.zeros((TILE, 128), F32), rows(c, where[p]), 0)
            if isinstance(c, int) and c in (3, 4):
                high, low = rows(FLUX, where[p])
                sub = lax.broadcasted_iota(jnp.int32, (TILE, 128), 0)
                tile = jnp.where(sub == (1 if c == 3 else TILE - 2), high if c == 3 else low, tile)
            if isinstance(c, int) and c >= 7:
                if p == 0:
                    tile = placed(placed(tile, rows(corner, c - 7), 1), rows(corner, c - 3), 2)
                if p == 1:
                    tile = placed(tile, rows(corner, c + 1), 1)
            return tile

        gather_plane(where[p], acts, g, vel, omega, solid, halo, lambda c: work.at[0, c, p] if c < 7 else st.at[c - 7, p], (right, sign))
        write_flags(st.at[3, p], fl.at[p])
    last = slice(ny, ny + TILE)
    msg[0, 0:ny] = work[0, 2, 0, 0:ny]
    msg[0, last] = placed(placed(work[0, 2, 0, last], rows(corner, 12), 1), rows(corner, 14), 2)
    msg[4] = st[0, 0] * sign
    for c in range(1, 4):
        msg[4 + c] = st[c, 0]
    msg[8] = st[3, 1] * (0.125 + st[0, 1])
    for t in range(1, 4):
        old, new = (t - 1) % 2, t % 2
        for p in range(4 - t):

            def pull_1(r, g2):
                if p == 0:
                    return jnp.zeros_like(g2)
                return work[old, 1, p - 1, r] + fl[p - 1, 5, r] * g2

            def pull_2(r, g1):
                return work[old, 2, p + 1, r] + fl[p + 1, 5, r] * g1

            def put(r, out, h):
                if t == 1 and r == last:
                    with_flux(out, h, rows, t, where[p])
                if p == 0:
                    msg[t, r] = placed(out[2], rows(corner, 13), 1) if t == 1 and r == last else out[2]
                if t < 3:
                    for c in range(7):
                        work[new, c, p, r] = out[c]

            gs = [work.at[old, c, p] for c in range(7)]
            advance(tiles, gs, pull_1, pull_2, [st.at[c, p] for c in range(3)], st.at[3, p], fl.at[p], put)


def interior(active, g, vel, omega, solid, rc, rd, out, near, ping, pong, stat, fl, mid, sem):
    y_even = even_index("gy")
    rc = rc.at[jnp.where(y_even, 1, 0)]
    nx, ny = omega.shape[0], omega.shape[1]
    tiles = ping.shape[2] // TILE
    acts = all_acts(active, ny)
    rows = halo_rows(rc, rd, y_even)
    for x in (0, nx + 1):
        for buf in (ping, pong):
            for c in (1, 2):
                buf[c, x] = jnp.zeros(buf.shape[2:], F32)
        fl[x, 5] = jnp.zeros(fl.shape[2:], F32)

    def build(x, _):
        def halo(c):
            tile = placed(jnp.zeros((TILE, 128), F32), rows(c, x), 0)
            sub = lax.broadcasted_iota(jnp.int32, (TILE, 128), 0)
            if c in (3, 4):
                high, low = rows(FLUX, x)
                tile = jnp.where(sub == (1 if c == 3 else TILE - 2), high if c == 3 else low, tile)
            if c == 10:
                tile = placed(tile, rows(FLUX + 3, x), 1)
            return tile

        gather_plane(x, acts, g, vel, omega, solid, halo, lambda c: ping.at[c, x + 1] if c < 7 else stat.at[c - 7, x], None)
        write_flags(stat.at[3, x], fl.at[x + 1])
        return 0

    lax.fori_loop(0, nx, build, 0, unroll=16)

    for t in range(ITERS):
        old, new = (ping, pong) if t % 2 == 0 else (pong, ping)

        def run(x, tiles, put):
            def pull_1(r, g2):
                return old[1, x + 2, r] + fl[x + 2, 5, r] * g2

            def pull_2(r, g1):
                return old[2, x, r] + fl[x, 5, r] * g1

            gs = [old.at[c, x + 1] for c in range(7)]
            advance(tiles, gs, pull_1, pull_2, [stat.at[c, x] for c in range(3)], stat.at[3, x], fl.at[x + 1], put)

        if t < ITERS - 1:

            def plane(x, _):
                def put(r, res, h):
                    if t < 2 and r.start == ny:
                        with_flux(res, h, rows, t + 1, x)
                    for c in range(7):
                        new[c, x + 1, r] = res[c]

                run(x, tiles, put)
                return 0

            lax.fori_loop(0, nx, plane, 0, unroll=16)
        else:

            def last(into, shift):
                def plane(x, _):
                    def put(r, res, h):
                        for c in range(7):
                            into[c, x - shift, r] = res[c]

                    run(x, ny // TILE, put)
                    return 0

                return plane

            lax.fori_loop(4, nx - 4, last(mid, 4), 0, unroll=4)
            store = pltpu.make_async_copy(mid, out.at[:, pl.ds(4, nx - 8)], sem.at[0])
            store.start()
            lax.fori_loop(0, 4, last(near, 0), 0, unroll=4)
            lax.fori_loop(nx - 4, nx, last(near, nx - 8), 0, unroll=4)
            store.wait()


def respond(which, mine, got, st, own, near, base, out, work, flags, hu1, done, sem):
    nx, ny = out.shape[1], out.shape[2]
    tiles = work.shape[3] // TILE
    right = even_index("gx") if which == 0 else jnp.logical_not(even_index("gx"))
    sign = jnp.where(right, 1.0, -1.0).astype(F32)
    theirs = got.at[jnp.where(right, 1, 0)] if which == 0 else got
    hu1[...] = theirs[4] * sign
    hu = {1: [hu1, theirs.at[5], theirs.at[6]]}
    a = {1: theirs.at[7]}
    fl = {0: flags.at[0], 1: flags.at[1]}
    for p in range(4):
        hu[2 + p] = [st.at[c, p] for c in range(3)]
        a[2 + p] = st.at[3, p]
        fl[2 + p] = own.at[p]
    write_flags(a[1], fl[1])
    fl[0][5] = jnp.where(theirs[8] > 0.0, 0.0, 1.0).astype(F32)
    live = set()
    stores = []
    for t in range(ITERS):
        old, new = t % 2, (t + 1) % 2
        todo = ((1, 2), (0, 1, 2, 3), (1, 2, 3, 4), (5, 4, 3, 2))[t]
        for q in todo:
            if q == 0:
                work[new, 1, 0] = theirs[8] * work[old, 2, 1]
                continue

            def pull_1(r, g2):
                h = fl[q - 1][5, r] * g2 if q in live else g2
                if q - 1 in live:
                    h = h + work[old, 1, q - 1, r]
                if q == 2:
                    h = h + (theirs[t, r] + fl[1][5, r] * mine[t, r])
                return h

            def pull_2(r, g1):
                h = fl[q + 1][5, r] * g1 if q in live else g1
                if q + 1 in live:
                    h = h + work[old, 2, q + 1, r]
                if q == 1:
                    h = h + (mine[t, r] + fl[2][5, r] * theirs[t, r])
                return h

            p = q - 2
            x = jnp.where(right, 7 - p, p)

            def put(r, res, h):
                if t < ITERS - 1:
                    for c in range(7):
                        work[new, c, q, r] = res[c]
                    return
                for c in range(7):
                    real = c if c not in (1, 2) else jnp.where(right, c, 3 - c)
                    done[p, real, r] = near[real, x, r] + res[c]

            gs = [work.at[old, c, q] for c in range(7)] if q in live else None
            advance(tiles if t < ITERS - 1 else ny // TILE, gs, pull_1, pull_2, hu[q], a[q], fl[q], put)
            if t == ITERS - 1:
                stores.append(pltpu.make_async_copy(done.at[p], out.at[:, jnp.where(right, nx - 1 - p, p)], sem.at[p]))
                stores[-1].start()
        live = set(todo)
    for store in stores:
        store.wait()


def pair_up(x, axis, first):
    pairs = []
    for i in range(first, lax.axis_size(axis) - 1, 2):
        pairs += [(i, i + 1), (i + 1, i)]
    return lax.ppermute(x, axis, pairs)


def call(kernel, outs, ins, out_specs, scratch, mib, cost, **more):
    return pl.pallas_call(
        kernel,
        out_shape=outs,
        in_specs=ins,
        out_specs=out_specs,
        scratch_shapes=scratch,
        compiler_params=params(mib),
        cost_estimate=pl.CostEstimate(flops=cost, bytes_accessed=4 * MIB, transcendentals=0),
        **more,
    )


def on_device(sensitivity, velocity, omega, solid, active):
    nx, ny, nz = omega.shape
    rows = ny + TILE
    f32 = lambda *shape: jax.ShapeDtypeStruct(shape, F32)
    vm = pltpu.VMEM
    dma = pltpu.SemaphoreType.DMA

    pinned = [pltpu.with_memory_space_constraint(v, pltpu.HBM) for v in (active, sensitivity, velocity, omega, solid)]
    edge = lambda *shape: vm((2,) + shape + (TILE, nz), F32)
    msg_c, msg_d = call(
        pack_rows,
        (f32(ROWS, nx, 1, nz),) * 2,
        [HBM, HBM, HBM, HBM, HBM],
        (VM,) * 2,
        [edge(7, nx), edge(3, nx), edge(nx), vm((2, nx, TILE, nz), jnp.int32), vm(active.shape, jnp.int32), edge(7, nx + 2), edge(7, nx + 2), edge(4, nx), edge(nx + 2, 6), dma((3, 4))],
        24,
        1 << 20,
    )(*pinned)
    rec_d = pair_up(msg_d, "gy", 1)
    rec_c = lax.all_gather(msg_c, "gy", axis_index_groups=[[i, i + 1] for i in range(0, lax.axis_size("gy"), 2)])

    def message(which, *after):
        return call(
            functools.partial(face, which),
            (f32(PARTS, rows, nz), f32(4, 4, rows, nz), f32(4, 6, rows, nz)),
            [VM, VM, VM, VM, VM, VM, VM] + [HBM] * len(after),
            (VM, VM, VM),
            [vm((2, 7, 4, rows, nz), F32)],
            24,
            1 << 20,
        )(active, sensitivity, velocity, omega, solid, rec_c, rec_d, *after)

    msg_b, st_b, fl_b = message(1)
    rec_b = pair_up(msg_b, "gx", 1)
    base, near = call(
        interior,
        (f32(7, nx, ny, nz), f32(7, 8, ny, nz)),
        [VM, VM, VM, VM, VM, VM, VM],
        (HBM, VM),
        [
            vm((7, nx + 2, rows, nz), F32),
            vm((7, nx + 2, rows, nz), F32),
            vm((4, nx, rows, nz), F32),
            vm((nx + 2, 6, rows, nz), F32),
            vm((7, nx - 8, ny, nz), F32),
            dma((1,)),
        ],
        32,
        1 << 24,
    )(active, sensitivity, velocity, omega, solid, rec_c, rec_d)

    msg_a, st_a, fl_a = message(0, msg_b)
    pairs = [[i, i + 1] for i in range(0, lax.axis_size("gx"), 2)]
    rec_a = lax.all_gather(msg_a, "gx", axis_index_groups=pairs)

    def corrected(which, mine, theirs, st, fl, base):
        return call(
            functools.partial(respond, which),
            f32(7, nx, ny, nz),
            [VM] * 5 + [HBM],
            HBM,
            [vm((2, 7, 6, rows, nz), F32), vm((2, 6, rows, nz), F32), vm((rows, nz), F32), vm((4, 7, ny, nz), F32), dma((4,))],
            24,
            1 << 20,
            input_output_aliases={5: 0},
        )(mine, theirs, st, fl, near, base)

    base = corrected(0, msg_a, rec_a, st_a, fl_a, base)
    return corrected(1, msg_b, rec_b, st_b, fl_b, base)


def solution(mesh):
    in_specs = (
        P(None, "gx", "gy", None),
        P(None, "gx", "gy", None),
        P("gx", "gy", None),
        P("gx", "gy", None),
        P("gx", "gy", None),
    )
    out_specs = P(None, "gx", "gy", None)
    return jax.shard_map(
        on_device, mesh=mesh, in_specs=in_specs, out_specs=out_specs, check_vma=False
    )
```

```python
import functools

import jax
import jax.numpy as jnp
from jax import lax
from jax.experimental import pallas as pl
from jax.experimental.pallas import tpu as pltpu
from jax.sharding import PartitionSpec as P

BLOCK = 16
ITERS = 4
TILE = 8
FIELDS = 11
FLUX = FIELDS
CORNER = FIELDS + 4
ROWS = CORNER + 2
PARTS = 9
SHARED = ((7, 2, 2), (0, 8, 2), (1, 4, 4), (5, 6, 4))
F32 = jnp.float32
MIB = 1 << 20

VM = pl.BlockSpec(memory_space=pltpu.VMEM)
HBM = pl.BlockSpec(memory_space=pl.ANY)


def params(mib):
    return pltpu.CompilerParams(vmem_limit_bytes=mib * MIB)


def even_index(axis):
    return lax.axis_index(axis) % 2 == 0


def lane_blocks(active, row, shape):
    lane = lax.broadcasted_iota(jnp.int32, shape, 1) // BLOCK
    out = jnp.zeros(shape, jnp.int32)
    for k in range(active.shape[1]):
        out = jnp.where(lane == k, jnp.broadcast_to(active[row:row + 1, k:k + 1], shape), out)
    return out


def rolled(v, step, axis):
    n = v.shape[axis]
    return pltpu.roll(v, (n - step) % n, axis)


def shift_z(v, step, fill):
    lane = lax.broadcasted_iota(jnp.int32, v.shape, 1)
    edge = v.shape[1] - 1 if step > 0 else 0
    return jnp.where(lane == edge, fill, rolled(v, step, 1))


def collide(h, hu, a, bc):
    s = 0.25 * h[0] + 0.125 * ((h[1] + h[2]) + (h[3] + h[4]) + (h[5] + h[6]))
    s = s + hu[0] * (h[1] - h[2]) + hu[1] * (h[3] - h[4]) + hu[2] * (h[5] - h[6])
    t = a * s
    return [t + bc * one for one in h]


def write_flags(a_ref, flags):
    a = a_ref[...]
    nf = jnp.where(a > 0.0, 0.0, 1.0).astype(F32)
    flags[0] = rolled(nf, 1, 0)
    flags[1] = rolled(nf, -1, 0)
    flags[2] = shift_z(nf, 1, 1.0)
    flags[3] = shift_z(nf, -1, 1.0)
    flags[4] = (1.0 - nf) - a
    flags[5] = nf


def advance(tiles, g, pull_1, pull_2, hu, a, flags, put, drop=None):
    if g is not None:
        g3, g4 = g[3][...], g[4][...]
        up, down = rolled(g3, 1, 0), rolled(g4, -1, 0)
    for i in range(tiles):
        r = slice(TILE * i, TILE * i + TILE)
        if g is None:
            zero = jnp.zeros((TILE, a.shape[1]), F32)
            h = [zero, pull_1(r, zero), pull_2(r, zero), zero, zero, zero, zero]
        else:
            g1, g2, g5, g6 = (g[c][r] for c in (1, 2, 5, 6))
            h = [
                g[0][r],
                pull_1(r, g2),
                pull_2(r, g1),
                up[r] + flags[0, r] * g4[r],
                down[r] + flags[1, r] * g3[r],
                shift_z(g5, 1, 0.0) + flags[2, r] * g6,
                shift_z(g6, -1, 0.0) + flags[3, r] * g5,
            ]
        if drop is not None:
            h[drop] = jnp.zeros_like(h[drop])
        put(r, collide(h, [one[r] for one in hu], a[r], flags[4, r]), h)


def pack_rows(active, g, vel, omega, solid, msg_c, msg_d, gb, vb, ob, sb, ab, ping, pong, stat, fl, sem):
    is_even = even_index("gy")
    nx, ny = omega.shape[0], omega.shape[1]
    copies = []
    for side in range(2):
        row = (ny - TILE // 2) * side
        half = pl.ds(TILE // 2 * side, TILE // 2)
        for n, (src, dst) in enumerate(((solid, sb), (omega, ob), (vel, vb), (g, gb))):
            at = pl.ds(row, TILE // 2)
            if len(src.shape) == 4:
                window, into = src.at[:, :, at, :], dst.at[side, :, :, half, :]
            else:
                window, into = src.at[:, at, :], dst.at[side, :, half, :]
            copies.append(pltpu.make_async_copy(window, into, sem.at[side, n]))
    copies.append(pltpu.make_async_copy(active, ab, sem.at[2, 0]))
    for copy in reversed(copies):
        copy.start()
    zero = jnp.zeros((TILE, 128), F32)
    for side in range(2):
        for x in (0, nx + 1):
            fl[side, x, 5] = zero
            for c in (1, 2):
                ping[side, c, x] = zero
                pong[side, c, x] = zero
    copies[-1].wait()
    acts = [lane_blocks(ab[0], (active.shape[1] - 1) * side, (TILE, 128)) for side in range(2)]
    for copy in copies[:-1]:
        copy.wait()

    def send(k, x, values, row):
        low, high = values[0][row:row + 1], values[1][TILE - 1 - row:TILE - row]
        msg_c[k, x] = jnp.where(is_even, high, low)
        msg_d[k, x] = jnp.where(is_even, low, high)

    def build(x, _):
        fields = []
        for side in range(2):
            f = ((1 - sb[side, x]) * acts[side]).astype(F32)
            vals = [gb[side, c, x] * f for c in range(7)] + [0.5 * vb[side, c, x] for c in range(3)] + [f * ob[side, x]]
            for c in range(FIELDS):
                if c < 7:
                    ping[side, c, x + 1] = vals[c]
                else:
                    stat[side, c - 7, x] = vals[c]
            write_flags(stat.at[side, 3, x], fl.at[side, x + 1])
            fields.append(vals)
        for c in range(FIELDS):
            send(c, x, [fields[0][c], fields[1][c]], 0)
        send(FLUX, x, [fields[0][3], fields[1][4]], 1)
        send(FLUX + 3, x, [fields[0][10] * (0.125 - fields[0][8]), fields[1][10] * (0.125 + fields[1][8])], 1)
        return 0

    lax.fori_loop(0, nx, build, 0, unroll=16)

    def step(x, t):
        old, new = (ping, pong) if t == 0 else (pong, ping)
        fluxes = []
        for side in range(2):

            def pull_1(r, g2):
                return old[side, 1, x + 2, r] + fl[side, x + 2, 5, r] * g2

            def pull_2(r, g1):
                return old[side, 2, x, r] + fl[side, x, 5, r] * g1

            def put(r, res, h):
                if t == 0:
                    for c in range(7):
                        new[side, c, x + 1, r] = res[c]
                fluxes.append(res[3 + side])

            gs = [old.at[side, c, x + 1] for c in range(7)]
            advance(1, gs, pull_1, pull_2, [stat.at[side, c, x] for c in range(3)], stat.at[side, 3, x], fl.at[side, x + 1], put, None if t == 0 else 4 - side)
        send(FLUX + 1 + t, x, fluxes, 1)

    for t in range(2):

        def plane(x, _):
            step(x, t)
            return 0

        lax.fori_loop(0, nx, plane, 0, unroll=16)

    for face in range(2):
        at = [nx - 1 if face else 0, nx - 2 if face else 1]
        for n, (p, row) in enumerate(((0, 1), (0, 2), (1, 1))):
            for c in range(4):
                send(CORNER + face, 4 * n + c, [stat[side, c, at[p]] for side in range(2)], row)
        for n, (buf, row) in enumerate(((None, 1), (pong, 1), (None, 2))):
            if buf is None:
                f = [((1 - sb[side, at[0]]) * acts[side]).astype(F32) for side in range(2)]
                send(CORNER + face, 12 + n, [gb[side, 1 + face, at[0]] * f[side] for side in range(2)], row)
            else:
                send(CORNER + face, 12 + n, [buf[side, 1 + face, at[0] + 1] for side in range(2)], row)
        msg_c[CORNER + face, 15] = zero[:1]
        msg_d[CORNER + face, 15] = zero[:1]


def halo_rows(rc, rd, y_even):
    def row(k, x):
        one, two = rc[k, x], rd[k, x]
        return jnp.where(y_even, one, two), jnp.where(y_even, two, one)

    return row


def placed(tile, rows, at):
    sub = lax.broadcasted_iota(jnp.int32, (TILE, 128), 0)
    return jnp.where(sub == at, rows[0], jnp.where(sub == TILE - 1 - at, rows[1], tile))


def with_flux(res, h, rows, t, x):
    sub = lax.broadcasted_iota(jnp.int32, (TILE, 128), 0)
    high, low = rows(FLUX + t, x)
    if t == 2:
        k = rows(FLUX + 3, x)
        high, low = high + k[0] * h[4], low + k[1] * h[3]
    res[3] = jnp.where(sub == 1, high, res[3])
    res[4] = jnp.where(sub == TILE - 2, low, res[4])


def all_acts(active, ny):
    nb = active.shape[1]
    return [lane_blocks(active[0], n, (ny // nb, 128)) for n in range(nb)]


def gather_plane(x, acts, g, vel, omega, solid, halo, dest, mirror):
    ny = omega.shape[1]
    half = ny // len(acts)
    f = jnp.concatenate([((1 - solid[x, n * half:(n + 1) * half]) * act).astype(F32) for n, act in enumerate(acts)], axis=0)
    for c in range(FIELDS):
        real = c
        if mirror is not None and c in (1, 2):
            real = jnp.where(mirror[0], c, 3 - c)
        own = g[real, x] * f if c < 7 else 0.5 * vel[c - 7, x] if c < 10 else f * omega[x]
        rest = halo(real)
        if mirror is not None and c == 7:
            own, rest = own * mirror[1], rest * mirror[1]
        to = dest(c)
        to[0:ny] = own
        to[ny:ny + TILE] = rest


def face(which, active, g, vel, omega, solid, rc, rd, *rest):
    msg, flux, st, fl, work = rest[-5:]
    y_even, x_even = even_index("gy"), even_index("gx")
    rc = rc.at[jnp.where(y_even, 1, 0)]
    nx, ny = omega.shape[0], omega.shape[1]
    tiles = work.shape[3] // TILE
    right = x_even if which == 0 else jnp.logical_not(x_even)
    sign = jnp.where(right, 1.0, -1.0).astype(F32)
    acts = all_acts(active, ny)
    rows = halo_rows(rc, rd, y_even)
    corner = jnp.where(right, CORNER + 1, CORNER)
    where = [jnp.where(right, nx - 1 - p, p) for p in range(4)]
    for p in range(4):

        def halo(c):
            tile = placed(jnp.zeros((TILE, 128), F32), rows(c, where[p]), 0)
            if isinstance(c, int) and c in (3, 4):
                high, low = rows(FLUX, where[p])
                sub = lax.broadcasted_iota(jnp.int32, (TILE, 128), 0)
                tile = jnp.where(sub == (1 if c == 3 else TILE - 2), high if c == 3 else low, tile)
            if isinstance(c, int) and c >= 7:
                if p == 0:
                    tile = placed(placed(tile, rows(corner, c - 7), 1), rows(corner, c - 3), 2)
                if p == 1:
                    tile = placed(tile, rows(corner, c + 1), 1)
            return tile

        gather_plane(where[p], acts, g, vel, omega, solid, halo, lambda c: work.at[0, c, p] if c < 7 else st.at[c - 7, p], (right, sign))
        write_flags(st.at[3, p], fl.at[p])
    last = slice(ny, ny + TILE)
    flux[0, 0:ny] = work[0, 2, 0, 0:ny]
    flux[0, last] = placed(placed(work[0, 2, 0, last], rows(corner, 12), 1), rows(corner, 14), 2)
    for t in range(1, 4):
        old, new = (t - 1) % 2, t % 2
        for p in range(4 - t):

            def pull_1(r, g2):
                if p == 0:
                    return jnp.zeros_like(g2)
                return work[old, 1, p - 1, r] + fl[p - 1, 5, r] * g2

            def pull_2(r, g1):
                return work[old, 2, p + 1, r] + fl[p + 1, 5, r] * g1

            def put(r, out, h):
                if t == 1 and r == last:
                    with_flux(out, h, rows, t, where[p])
                if p == 0:
                    flux[t, r] = placed(out[2], rows(corner, 13), 1) if t == 1 and r == last else out[2]
                if t < 3:
                    for c in range(7):
                        work[new, c, p, r] = out[c]

            gs = [work.at[old, c, p] for c in range(7)]
            advance(tiles, gs, pull_1, pull_2, [st.at[c, p] for c in range(3)], st.at[3, p], fl.at[p], put)

    def part(k, r):
        if k < 4:
            return flux[k, r]
        if k < 8:
            return st[0, 0, r] * sign if k == 4 else st[k - 4, 0, r]
        return st[3, 1, r] * (0.125 + st[0, 1, r])

    for k in range(PARTS):
        for i in range(ny // TILE):
            msg[k * (ny // TILE) + i] = part(k, slice(TILE * i, TILE * i + TILE))
    for n, (one, two, width) in enumerate(SHARED):
        msg[PARTS * (ny // TILE) + n] = between(part(two, last), part(one, last), width)


def between(two, one, width):
    sub = lax.broadcasted_iota(jnp.int32, (TILE, 128), 0)
    middle = (sub >= (TILE - width) // 2) & (sub < (TILE + width) // 2)
    return jnp.where(middle, pltpu.roll(two, TILE // 2, 0), one)


def unpacked(msg, parts):
    tiles = parts.shape[1] // TILE - 1
    last = slice(tiles * TILE, tiles * TILE + TILE)
    for k in range(PARTS):
        for i in range(tiles):
            parts[k, TILE * i:TILE * i + TILE] = msg[k * tiles + i]
    for n, (one, two, _) in enumerate(SHARED):
        tile = msg[PARTS * tiles + n]
        parts[one, last] = tile
        parts[two, last] = pltpu.roll(tile, TILE // 2, 0)
    parts[3, last] = jnp.zeros((TILE, 128), F32)


def interior(active, g, vel, omega, solid, rc, rd, out, near, ping, pong, stat, fl, mid, sem):
    y_even = even_index("gy")
    rc = rc.at[jnp.where(y_even, 1, 0)]
    nx, ny = omega.shape[0], omega.shape[1]
    tiles = ping.shape[2] // TILE
    acts = all_acts(active, ny)
    rows = halo_rows(rc, rd, y_even)
    for x in (0, nx + 1):
        for buf in (ping, pong):
            for c in (1, 2):
                buf[c, x] = jnp.zeros(buf.shape[2:], F32)
        fl[x, 5] = jnp.zeros(fl.shape[2:], F32)

    def build(x, _):
        def halo(c):
            tile = placed(jnp.zeros((TILE, 128), F32), rows(c, x), 0)
            sub = lax.broadcasted_iota(jnp.int32, (TILE, 128), 0)
            if c in (3, 4):
                high, low = rows(FLUX, x)
                tile = jnp.where(sub == (1 if c == 3 else TILE - 2), high if c == 3 else low, tile)
            if c == 10:
                tile = placed(tile, rows(FLUX + 3, x), 1)
            return tile

        gather_plane(x, acts, g, vel, omega, solid, halo, lambda c: ping.at[c, x + 1] if c < 7 else stat.at[c - 7, x], None)
        write_flags(stat.at[3, x], fl.at[x + 1])
        return 0

    lax.fori_loop(0, nx, build, 0, unroll=16)

    for t in range(ITERS):
        old, new = (ping, pong) if t % 2 == 0 else (pong, ping)

        def run(x, tiles, put):
            def pull_1(r, g2):
                return old[1, x + 2, r] + fl[x + 2, 5, r] * g2

            def pull_2(r, g1):
                return old[2, x, r] + fl[x, 5, r] * g1

            gs = [old.at[c, x + 1] for c in range(7)]
            advance(tiles, gs, pull_1, pull_2, [stat.at[c, x] for c in range(3)], stat.at[3, x], fl.at[x + 1], put)

        if t < ITERS - 1:

            def plane(x, _):
                def put(r, res, h):
                    if t < 2 and r.start == ny:
                        with_flux(res, h, rows, t + 1, x)
                    for c in range(7):
                        new[c, x + 1, r] = res[c]

                run(x, tiles, put)
                return 0

            lax.fori_loop(0, nx, plane, 0, unroll=16)
        else:

            def last(into, shift):
                def plane(x, _):
                    def put(r, res, h):
                        for c in range(7):
                            into[c, x - shift, r] = res[c]

                    run(x, ny // TILE, put)
                    return 0

                return plane

            lax.fori_loop(4, nx - 4, last(mid, 4), 0, unroll=4)
            store = pltpu.make_async_copy(mid, out.at[:, pl.ds(4, nx - 8)], sem.at[0])
            store.start()
            lax.fori_loop(0, 4, last(near, 0), 0, unroll=4)
            lax.fori_loop(nx - 4, nx, last(near, nx - 8), 0, unroll=4)
            store.wait()


def respond(which, mine, got, st, own, near, base, out, work, flags, hu1, theirs, done, sem):
    nx, ny = out.shape[1], out.shape[2]
    tiles = work.shape[3] // TILE
    right = even_index("gx") if which == 0 else jnp.logical_not(even_index("gx"))
    sign = jnp.where(right, 1.0, -1.0).astype(F32)
    unpacked(got.at[jnp.where(right, 1, 0)] if which == 0 else got, theirs)
    hu1[...] = theirs[4] * sign
    hu = {1: [hu1, theirs.at[5], theirs.at[6]]}
    a = {1: theirs.at[7]}
    fl = {0: flags.at[0], 1: flags.at[1]}
    for p in range(4):
        hu[2 + p] = [st.at[c, p] for c in range(3)]
        a[2 + p] = st.at[3, p]
        fl[2 + p] = own.at[p]
    write_flags(a[1], fl[1])
    fl[0][5] = jnp.where(theirs[8] > 0.0, 0.0, 1.0).astype(F32)
    live = set()
    stores = []
    for t in range(ITERS):
        old, new = t % 2, (t + 1) % 2
        todo = ((1, 2), (0, 1, 2, 3), (1, 2, 3, 4), (5, 4, 3, 2))[t]
        for q in todo:
            if q == 0:
                work[new, 1, 0] = theirs[8] * work[old, 2, 1]
                continue

            def pull_1(r, g2):
                h = fl[q - 1][5, r] * g2 if q in live else g2
                if q - 1 in live:
                    h = h + work[old, 1, q - 1, r]
                if q == 2:
                    h = h + (theirs[t, r] + fl[1][5, r] * mine[t, r])
                return h

            def pull_2(r, g1):
                h = fl[q + 1][5, r] * g1 if q in live else g1
                if q + 1 in live:
                    h = h + work[old, 2, q + 1, r]
                if q == 1:
                    h = h + (mine[t, r] + fl[2][5, r] * theirs[t, r])
                return h

            p = q - 2
            x = jnp.where(right, 7 - p, p)

            def put(r, res, h):
                if t < ITERS - 1:
                    for c in range(7):
                        work[new, c, q, r] = res[c]
                    return
                for c in range(7):
                    real = c if c not in (1, 2) else jnp.where(right, c, 3 - c)
                    done[p, real, r] = near[real, x, r] + res[c]

            gs = [work.at[old, c, q] for c in range(7)] if q in live else None
            advance(tiles if t < ITERS - 1 else ny // TILE, gs, pull_1, pull_2, hu[q], a[q], fl[q], put)
            if t == ITERS - 1:
                stores.append(pltpu.make_async_copy(done.at[p], out.at[:, jnp.where(right, nx - 1 - p, p)], sem.at[p]))
                stores[-1].start()
        live = set(todo)
    for store in stores:
        store.wait()


def pair_up(x, axis, first):
    pairs = []
    for i in range(first, lax.axis_size(axis) - 1, 2):
        pairs += [(i, i + 1), (i + 1, i)]
    return lax.ppermute(x, axis, pairs)


def call(kernel, outs, ins, out_specs, scratch, mib, cost, **more):
    return pl.pallas_call(
        kernel,
        out_shape=outs,
        in_specs=ins,
        out_specs=out_specs,
        scratch_shapes=scratch,
        compiler_params=params(mib),
        cost_estimate=pl.CostEstimate(flops=cost, bytes_accessed=4 * MIB, transcendentals=0),
        **more,
    )


def on_device(sensitivity, velocity, omega, solid, active):
    nx, ny, nz = omega.shape
    rows = ny + TILE
    f32 = lambda *shape: jax.ShapeDtypeStruct(shape, F32)
    vm = pltpu.VMEM
    dma = pltpu.SemaphoreType.DMA

    pinned = [pltpu.with_memory_space_constraint(v, pltpu.HBM) for v in (active, sensitivity, velocity, omega, solid)]
    edge = lambda *shape: vm((2,) + shape + (TILE, nz), F32)
    msg_c, msg_d = call(
        pack_rows,
        (f32(ROWS, nx, 1, nz),) * 2,
        [HBM, HBM, HBM, HBM, HBM],
        (VM,) * 2,
        [edge(7, nx), edge(3, nx), edge(nx), vm((2, nx, TILE, nz), jnp.int32), vm(active.shape, jnp.int32), edge(7, nx + 2), edge(7, nx + 2), edge(4, nx), edge(nx + 2, 6), dma((3, 4))],
        24,
        1 << 20,
    )(*pinned)
    rec_d = pair_up(msg_d, "gy", 1)
    rec_c = lax.all_gather(msg_c, "gy", axis_index_groups=[[i, i + 1] for i in range(0, lax.axis_size("gy"), 2)])

    def message(which, *after):
        return call(
            functools.partial(face, which),
            (f32(PARTS * (ny // TILE) + len(SHARED), TILE, nz), f32(4, rows, nz), f32(4, 4, rows, nz), f32(4, 6, rows, nz)),
            [VM, VM, VM, VM, VM, VM, VM] + [HBM] * len(after),
            (VM, VM, VM, VM),
            [vm((2, 7, 4, rows, nz), F32)],
            24,
            1 << 20,
        )(active, sensitivity, velocity, omega, solid, rec_c, rec_d, *after)

    msg_b, flux_b, st_b, fl_b = message(1)
    rec_b = pair_up(msg_b, "gx", 1)
    base, near = call(
        interior,
        (f32(7, nx, ny, nz), f32(7, 8, ny, nz)),
        [VM, VM, VM, VM, VM, VM, VM],
        (HBM, VM),
        [
            vm((7, nx + 2, rows, nz), F32),
            vm((7, nx + 2, rows, nz), F32),
            vm((4, nx, rows, nz), F32),
            vm((nx + 2, 6, rows, nz), F32),
            vm((7, nx - 8, ny, nz), F32),
            dma((1,)),
        ],
        32,
        1 << 24,
    )(active, sensitivity, velocity, omega, solid, rec_c, rec_d)

    msg_a, flux_a, st_a, fl_a = message(0, flux_b)
    pairs = [[i, i + 1] for i in range(0, lax.axis_size("gx"), 2)]
    rec_a = lax.all_gather(msg_a, "gx", axis_index_groups=pairs)

    def corrected(which, mine, theirs, st, fl, base):
        return call(
            functools.partial(respond, which),
            f32(7, nx, ny, nz),
            [VM] * 5 + [HBM],
            HBM,
            [vm((2, 7, 6, rows, nz), F32), vm((2, 6, rows, nz), F32), vm((rows, nz), F32), vm((PARTS, rows, nz), F32), vm((4, 7, ny, nz), F32), dma((4,))],
            24,
            1 << 20,
            input_output_aliases={5: 0},
        )(mine, theirs, st, fl, near, base)

    base = corrected(0, flux_a, rec_a, st_a, fl_a, base)
    return corrected(1, flux_b, rec_b, st_b, fl_b, base)


def solution(mesh):
    in_specs = (
        P(None, "gx", "gy", None),
        P(None, "gx", "gy", None),
        P("gx", "gy", None),
        P("gx", "gy", None),
        P("gx", "gy", None),
    )
    out_specs = P(None, "gx", "gy", None)
    return jax.shard_map(
        on_device, mesh=mesh, in_specs=in_specs, out_specs=out_specs, check_vma=False
    )
```

```python
import functools

import jax
import jax.numpy as jnp
from jax import lax
from jax.experimental import pallas as pl
from jax.experimental.pallas import tpu as pltpu
from jax.sharding import PartitionSpec as P

BLOCK = 16
ITERS = 4
TILE = 8
FIELDS = 11
FLUX = FIELDS
CORNER = FIELDS + 4
ROWS = CORNER + 2
PARTS = 9
SHARED = ((7, 2, 2), (0, 8, 2), (1, 4, 4), (5, 6, 4))
F32 = jnp.float32
MIB = 1 << 20

VM = pl.BlockSpec(memory_space=pltpu.VMEM)
HBM = pl.BlockSpec(memory_space=pl.ANY)


def params(mib):
    return pltpu.CompilerParams(vmem_limit_bytes=mib * MIB)


def even_index(axis):
    return lax.axis_index(axis) % 2 == 0


def lane_blocks(active, row, shape):
    lane = lax.broadcasted_iota(jnp.int32, shape, 1) // BLOCK
    out = jnp.zeros(shape, jnp.int32)
    for k in range(active.shape[1]):
        out = jnp.where(lane == k, jnp.broadcast_to(active[row:row + 1, k:k + 1], shape), out)
    return out


def rolled(v, step, axis):
    n = v.shape[axis]
    return pltpu.roll(v, (n - step) % n, axis)


def shift_z(v, step, fill):
    lane = lax.broadcasted_iota(jnp.int32, v.shape, 1)
    edge = v.shape[1] - 1 if step > 0 else 0
    return jnp.where(lane == edge, fill, rolled(v, step, 1))


def collide(h, hu, a, bc):
    s = 0.25 * h[0] + 0.125 * ((h[1] + h[2]) + (h[3] + h[4]) + (h[5] + h[6]))
    s = s + hu[0] * (h[1] - h[2]) + hu[1] * (h[3] - h[4]) + hu[2] * (h[5] - h[6])
    t = a * s
    return [t + bc * one for one in h]


def write_flags(a_ref, flags):
    a = a_ref[...]
    nf = jnp.where(a > 0.0, 0.0, 1.0).astype(F32)
    flags[0] = rolled(nf, 1, 0)
    flags[1] = rolled(nf, -1, 0)
    flags[2] = shift_z(nf, 1, 1.0)
    flags[3] = shift_z(nf, -1, 1.0)
    flags[4] = (1.0 - nf) - a
    flags[5] = nf


def advance(tiles, g, pull_1, pull_2, hu, a, flags, put, drop=False):
    if g is not None:
        g3, g4 = g[3][...], g[4][...]
        up, down = rolled(g3, 1, 0), rolled(g4, -1, 0)
    for i in range(tiles):
        r = slice(TILE * i, TILE * i + TILE)
        if g is None:
            zero = jnp.zeros((TILE, a.shape[1]), F32)
            h = [zero, pull_1(r, zero), pull_2(r, zero), zero, zero, zero, zero]
        else:
            g1, g2, g5, g6 = (g[c][r] for c in (1, 2, 5, 6))
            h = [
                g[0][r],
                pull_1(r, g2),
                pull_2(r, g1),
                up[r] + flags[0, r] * g4[r],
                down[r] + flags[1, r] * g3[r],
                shift_z(g5, 1, 0.0) + flags[2, r] * g6,
                shift_z(g6, -1, 0.0) + flags[3, r] * g5,
            ]
        if drop:
            low = lax.broadcasted_iota(jnp.int32, h[3].shape, 0) < TILE // 2
            h[3], h[4] = jnp.where(low, h[3], 0.0), jnp.where(low, 0.0, h[4])
        put(r, collide(h, [one[r] for one in hu], a[r], flags[4, r]), h)


def pack_rows(active, g, vel, omega, solid, msg_c, msg_d, gb, vb, ob, sb, ab, ping, pong, stat, fl, sem):
    is_even = even_index("gy")
    nx, ny = omega.shape[0], omega.shape[1]
    half = TILE // 2
    copies = []
    for side in range(2):
        rows, into = pl.ds((ny - half) * side, half), pl.ds(half * side, half)
        for n, (src, dst) in enumerate(((solid, sb), (omega, ob), (vel, vb), (g, gb))):
            if len(src.shape) == 4:
                window = src.at[:, :, rows, :], dst.at[:, :, into, :]
            else:
                window = src.at[:, rows, :], dst.at[:, into, :]
            copies.append(pltpu.make_async_copy(*window, sem.at[side, n]))
    copies.append(pltpu.make_async_copy(active, ab, sem.at[2, 0]))
    for copy in reversed(copies):
        copy.start()
    shape = (TILE, 128)
    zero = jnp.zeros(shape, F32)
    for x in (0, nx + 1):
        fl[x, 5] = zero
        for c in (1, 2):
            ping[c, x] = zero
            pong[c, x] = zero
    copies[-1].wait()
    low = lax.broadcasted_iota(jnp.int32, shape, 0) < half
    act = jnp.where(low, lane_blocks(ab[0], 0, shape), lane_blocks(ab[0], active.shape[1] - 1, shape))
    for copy in copies[:-1]:
        copy.wait()

    def send(k, x, below, above, row):
        first, last = below[row:row + 1], above[TILE - 1 - row:TILE - row]
        msg_c[k, x] = jnp.where(is_even, last, first)
        msg_d[k, x] = jnp.where(is_even, first, last)

    def build(x, _):
        f = ((1 - sb[x]) * act).astype(F32)
        vals = [gb[c, x] * f for c in range(7)] + [0.5 * vb[c, x] for c in range(3)] + [f * ob[x]]
        for c in range(FIELDS):
            if c < 7:
                ping[c, x + 1] = vals[c]
            else:
                stat[c - 7, x] = vals[c]
            send(c, x, vals[c], vals[c], 0)
        write_flags(stat.at[3, x], fl.at[x + 1])
        send(FLUX, x, vals[3], vals[4], 1)
        send(FLUX + 3, x, vals[10] * (0.125 - vals[8]), vals[10] * (0.125 + vals[8]), 1)
        return 0

    lax.fori_loop(0, nx, build, 0, unroll=nx)

    def step(x, t):
        old, new = (ping, pong) if t == 0 else (pong, ping)

        def pull_1(r, g2):
            return old[1, x + 2, r] + fl[x + 2, 5, r] * g2

        def pull_2(r, g1):
            return old[2, x, r] + fl[x, 5, r] * g1

        def put(r, res, h):
            if t == 0:
                for c in range(7):
                    new[c, x + 1, r] = res[c]
            send(FLUX + 1 + t, x, res[3], res[4], 1)

        gs = [old.at[c, x + 1] for c in range(7)]
        advance(1, gs, pull_1, pull_2, [stat.at[c, x] for c in range(3)], stat.at[3, x], fl.at[x + 1], put, t == 1)

    for t in range(2):

        def plane(x, _):
            step(x, t)
            return 0

        lax.fori_loop(0, nx, plane, 0, unroll=nx)

    for face in range(2):
        at = [nx - 1 if face else 0, nx - 2 if face else 1]
        for n, (p, row) in enumerate(((0, 1), (0, 2), (1, 1))):
            for c in range(4):
                plane = stat[c, at[p]]
                send(CORNER + face, 4 * n + c, plane, plane, row)
        start = gb[1 + face, at[0]] * ((1 - sb[at[0]]) * act).astype(F32)
        after = pong[1 + face, at[0] + 1]
        send(CORNER + face, 12, start, start, 1)
        send(CORNER + face, 13, after, after, 1)
        send(CORNER + face, 14, start, start, 2)
        msg_c[CORNER + face, 15] = zero[:1]
        msg_d[CORNER + face, 15] = zero[:1]


def halo_rows(rc, rd, y_even):
    def row(k, x):
        one, two = rc[k, x], rd[k, x]
        return jnp.where(y_even, one, two), jnp.where(y_even, two, one)

    return row


def placed(tile, rows, at):
    sub = lax.broadcasted_iota(jnp.int32, (TILE, 128), 0)
    return jnp.where(sub == at, rows[0], jnp.where(sub == TILE - 1 - at, rows[1], tile))


def with_flux(res, h, rows, t, x):
    sub = lax.broadcasted_iota(jnp.int32, (TILE, 128), 0)
    high, low = rows(FLUX + t, x)
    if t == 2:
        k = rows(FLUX + 3, x)
        high, low = high + k[0] * h[4], low + k[1] * h[3]
    res[3] = jnp.where(sub == 1, high, res[3])
    res[4] = jnp.where(sub == TILE - 2, low, res[4])


def all_acts(active, ny):
    nb = active.shape[1]
    return [lane_blocks(active[0], n, (ny // nb, 128)) for n in range(nb)]


def gather_plane(x, acts, g, vel, omega, solid, halo, dest, mirror):
    ny = omega.shape[1]
    half = ny // len(acts)
    f = jnp.concatenate([((1 - solid[x, n * half:(n + 1) * half]) * act).astype(F32) for n, act in enumerate(acts)], axis=0)
    for c in range(FIELDS):
        real = c
        if mirror is not None and c in (1, 2):
            real = jnp.where(mirror[0], c, 3 - c)
        own = g[real, x] * f if c < 7 else 0.5 * vel[c - 7, x] if c < 10 else f * omega[x]
        rest = halo(real)
        if mirror is not None and c == 7:
            own, rest = own * mirror[1], rest * mirror[1]
        to = dest(c)
        to[0:ny] = own
        to[ny:ny + TILE] = rest


def face(which, active, g, vel, omega, solid, rc, rd, *rest):
    msg, flux, st, fl, work = rest[-5:]
    y_even, x_even = even_index("gy"), even_index("gx")
    rc = rc.at[jnp.where(y_even, 1, 0)]
    nx, ny = omega.shape[0], omega.shape[1]
    tiles = work.shape[3] // TILE
    right = x_even if which == 0 else jnp.logical_not(x_even)
    sign = jnp.where(right, 1.0, -1.0).astype(F32)
    acts = all_acts(active, ny)
    rows = halo_rows(rc, rd, y_even)
    corner = jnp.where(right, CORNER + 1, CORNER)
    where = [jnp.where(right, nx - 1 - p, p) for p in range(4)]
    for p in range(4):

        def halo(c):
            tile = placed(jnp.zeros((TILE, 128), F32), rows(c, where[p]), 0)
            if isinstance(c, int) and c in (3, 4):
                high, low = rows(FLUX, where[p])
                sub = lax.broadcasted_iota(jnp.int32, (TILE, 128), 0)
                tile = jnp.where(sub == (1 if c == 3 else TILE - 2), high if c == 3 else low, tile)
            if isinstance(c, int) and c >= 7:
                if p == 0:
                    tile = placed(placed(tile, rows(corner, c - 7), 1), rows(corner, c - 3), 2)
                if p == 1:
                    tile = placed(tile, rows(corner, c + 1), 1)
            return tile

        gather_plane(where[p], acts, g, vel, omega, solid, halo, lambda c: work.at[0, c, p] if c < 7 else st.at[c - 7, p], (right, sign))
        write_flags(st.at[3, p], fl.at[p])
    last = slice(ny, ny + TILE)
    flux[0, 0:ny] = work[0, 2, 0, 0:ny]
    flux[0, last] = placed(placed(work[0, 2, 0, last], rows(corner, 12), 1), rows(corner, 14), 2)
    for t in range(1, 4):
        old, new = (t - 1) % 2, t % 2
        for p in range(4 - t):

            def pull_1(r, g2):
                if p == 0:
                    return jnp.zeros_like(g2)
                return work[old, 1, p - 1, r] + fl[p - 1, 5, r] * g2

            def pull_2(r, g1):
                return work[old, 2, p + 1, r] + fl[p + 1, 5, r] * g1

            def put(r, out, h):
                if t == 1 and r == last:
                    with_flux(out, h, rows, t, where[p])
                if p == 0:
                    flux[t, r] = placed(out[2], rows(corner, 13), 1) if t == 1 and r == last else out[2]
                if t < 3:
                    for c in range(7):
                        work[new, c, p, r] = out[c]

            gs = [work.at[old, c, p] for c in range(7)]
            advance(tiles, gs, pull_1, pull_2, [st.at[c, p] for c in range(3)], st.at[3, p], fl.at[p], put)

    def part(k, r):
        if k < 4:
            return flux[k, r]
        if k < 8:
            return st[0, 0, r] * sign if k == 4 else st[k - 4, 0, r]
        return st[3, 1, r] * (0.125 + st[0, 1, r])

    for k in range(PARTS):
        for i in range(ny // TILE):
            msg[k * (ny // TILE) + i] = part(k, slice(TILE * i, TILE * i + TILE))
    for n, (one, two, width) in enumerate(SHARED):
        msg[PARTS * (ny // TILE) + n] = between(part(two, last), part(one, last), width)


def between(two, one, width):
    sub = lax.broadcasted_iota(jnp.int32, (TILE, 128), 0)
    middle = (sub >= (TILE - width) // 2) & (sub < (TILE + width) // 2)
    return jnp.where(middle, pltpu.roll(two, TILE // 2, 0), one)


def unpacked(msg, parts):
    tiles = parts.shape[1] // TILE - 1
    last = slice(tiles * TILE, tiles * TILE + TILE)
    for k in range(PARTS):
        for i in range(tiles):
            parts[k, TILE * i:TILE * i + TILE] = msg[k * tiles + i]
    for n, (one, two, _) in enumerate(SHARED):
        tile = msg[PARTS * tiles + n]
        parts[one, last] = tile
        parts[two, last] = pltpu.roll(tile, TILE // 2, 0)
    parts[3, last] = jnp.zeros((TILE, 128), F32)


def interior(active, g, vel, omega, solid, rc, rd, out, near, ping, pong, stat, fl, mid, sem):
    y_even = even_index("gy")
    rc = rc.at[jnp.where(y_even, 1, 0)]
    nx, ny = omega.shape[0], omega.shape[1]
    tiles = ping.shape[2] // TILE
    acts = all_acts(active, ny)
    rows = halo_rows(rc, rd, y_even)
    for x in (0, nx + 1):
        for buf in (ping, pong):
            for c in (1, 2):
                buf[c, x] = jnp.zeros(buf.shape[2:], F32)
        fl[x, 5] = jnp.zeros(fl.shape[2:], F32)

    def build(x, _):
        def halo(c):
            tile = placed(jnp.zeros((TILE, 128), F32), rows(c, x), 0)
            sub = lax.broadcasted_iota(jnp.int32, (TILE, 128), 0)
            if c in (3, 4):
                high, low = rows(FLUX, x)
                tile = jnp.where(sub == (1 if c == 3 else TILE - 2), high if c == 3 else low, tile)
            if c == 10:
                tile = placed(tile, rows(FLUX + 3, x), 1)
            return tile

        gather_plane(x, acts, g, vel, omega, solid, halo, lambda c: ping.at[c, x + 1] if c < 7 else stat.at[c - 7, x], None)
        write_flags(stat.at[3, x], fl.at[x + 1])
        return 0

    lax.fori_loop(0, nx, build, 0, unroll=16)

    for t in range(ITERS):
        old, new = (ping, pong) if t % 2 == 0 else (pong, ping)

        def run(x, tiles, put):
            def pull_1(r, g2):
                return old[1, x + 2, r] + fl[x + 2, 5, r] * g2

            def pull_2(r, g1):
                return old[2, x, r] + fl[x, 5, r] * g1

            gs = [old.at[c, x + 1] for c in range(7)]
            advance(tiles, gs, pull_1, pull_2, [stat.at[c, x] for c in range(3)], stat.at[3, x], fl.at[x + 1], put)

        if t < ITERS - 1:

            def plane(x, _):
                def put(r, res, h):
                    if t < 2 and r.start == ny:
                        with_flux(res, h, rows, t + 1, x)
                    for c in range(7):
                        new[c, x + 1, r] = res[c]

                run(x, tiles, put)
                return 0

            lax.fori_loop(0, nx, plane, 0, unroll=16)
        else:

            def last(into, shift):
                def plane(x, _):
                    def put(r, res, h):
                        for c in range(7):
                            into[c, x - shift, r] = res[c]

                    run(x, ny // TILE, put)
                    return 0

                return plane

            lax.fori_loop(4, nx - 4, last(mid, 4), 0, unroll=4)
            store = pltpu.make_async_copy(mid, out.at[:, pl.ds(4, nx - 8)], sem.at[0])
            store.start()
            lax.fori_loop(0, 4, last(near, 0), 0, unroll=4)
            lax.fori_loop(nx - 4, nx, last(near, nx - 8), 0, unroll=4)
            store.wait()


def respond(which, mine, got, st, own, near, base, out, work, flags, hu1, theirs, done, sem):
    nx, ny = out.shape[1], out.shape[2]
    tiles = work.shape[3] // TILE
    right = even_index("gx") if which == 0 else jnp.logical_not(even_index("gx"))
    sign = jnp.where(right, 1.0, -1.0).astype(F32)
    unpacked(got.at[jnp.where(right, 1, 0)] if which == 0 else got, theirs)
    hu1[...] = theirs[4] * sign
    hu = {1: [hu1, theirs.at[5], theirs.at[6]]}
    a = {1: theirs.at[7]}
    fl = {0: flags.at[0], 1: flags.at[1]}
    for p in range(4):
        hu[2 + p] = [st.at[c, p] for c in range(3)]
        a[2 + p] = st.at[3, p]
        fl[2 + p] = own.at[p]
    write_flags(a[1], fl[1])
    fl[0][5] = jnp.where(theirs[8] > 0.0, 0.0, 1.0).astype(F32)
    live = set()
    stores = []
    for t in range(ITERS):
        old, new = t % 2, (t + 1) % 2
        todo = ((1, 2), (0, 1, 2, 3), (1, 2, 3, 4), (5, 4, 3, 2))[t]
        for q in todo:
            if q == 0:
                work[new, 1, 0] = theirs[8] * work[old, 2, 1]
                continue

            def pull_1(r, g2):
                h = fl[q - 1][5, r] * g2 if q in live else g2
                if q - 1 in live:
                    h = h + work[old, 1, q - 1, r]
                if q == 2:
                    h = h + (theirs[t, r] + fl[1][5, r] * mine[t, r])
                return h

            def pull_2(r, g1):
                h = fl[q + 1][5, r] * g1 if q in live else g1
                if q + 1 in live:
                    h = h + work[old, 2, q + 1, r]
                if q == 1:
                    h = h + (mine[t, r] + fl[2][5, r] * theirs[t, r])
                return h

            p = q - 2
            x = jnp.where(right, 7 - p, p)

            def put(r, res, h):
                if t < ITERS - 1:
                    for c in range(7):
                        work[new, c, q, r] = res[c]
                    return
                for c in range(7):
                    real = c if c not in (1, 2) else jnp.where(right, c, 3 - c)
                    done[p, real, r] = near[real, x, r] + res[c]

            gs = [work.at[old, c, q] for c in range(7)] if q in live else None
            advance(tiles if t < ITERS - 1 else ny // TILE, gs, pull_1, pull_2, hu[q], a[q], fl[q], put)
            if t == ITERS - 1:
                stores.append(pltpu.make_async_copy(done.at[p], out.at[:, jnp.where(right, nx - 1 - p, p)], sem.at[p]))
                stores[-1].start()
        live = set(todo)
    for store in stores:
        store.wait()


def pair_up(x, axis, first):
    pairs = []
    for i in range(first, lax.axis_size(axis) - 1, 2):
        pairs += [(i, i + 1), (i + 1, i)]
    return lax.ppermute(x, axis, pairs)


def call(kernel, outs, ins, out_specs, scratch, mib, cost, **more):
    return pl.pallas_call(
        kernel,
        out_shape=outs,
        in_specs=ins,
        out_specs=out_specs,
        scratch_shapes=scratch,
        compiler_params=params(mib),
        cost_estimate=pl.CostEstimate(flops=cost, bytes_accessed=4 * MIB, transcendentals=0),
        **more,
    )


def on_device(sensitivity, velocity, omega, solid, active):
    nx, ny, nz = omega.shape
    rows = ny + TILE
    f32 = lambda *shape: jax.ShapeDtypeStruct(shape, F32)
    vm = pltpu.VMEM
    dma = pltpu.SemaphoreType.DMA

    pinned = [pltpu.with_memory_space_constraint(v, pltpu.HBM) for v in (active, sensitivity, velocity, omega, solid)]
    edge = lambda *shape: vm(shape + (TILE, nz), F32)
    msg_c, msg_d = call(
        pack_rows,
        (f32(ROWS, nx, 1, nz),) * 2,
        [HBM, HBM, HBM, HBM, HBM],
        (VM,) * 2,
        [edge(7, nx), edge(3, nx), edge(nx), vm((nx, TILE, nz), jnp.int32), vm(active.shape, jnp.int32), edge(7, nx + 2), edge(7, nx + 2), edge(4, nx), edge(nx + 2, 6), dma((3, 4))],
        24,
        1 << 20,
    )(*pinned)
    rec_d = pair_up(msg_d, "gy", 1)
    rec_c = lax.all_gather(msg_c, "gy", axis_index_groups=[[i, i + 1] for i in range(0, lax.axis_size("gy"), 2)])

    def message(which, *after):
        return call(
            functools.partial(face, which),
            (f32(PARTS * (ny // TILE) + len(SHARED), TILE, nz), f32(4, rows, nz), f32(4, 4, rows, nz), f32(4, 6, rows, nz)),
            [VM, VM, VM, VM, VM, VM, VM] + [HBM] * len(after),
            (VM, VM, VM, VM),
            [vm((2, 7, 4, rows, nz), F32)],
            24,
            1 << 20,
        )(active, sensitivity, velocity, omega, solid, rec_c, rec_d, *after)

    msg_b, flux_b, st_b, fl_b = message(1)
    rec_b = pair_up(msg_b, "gx", 1)
    base, near = call(
        interior,
        (f32(7, nx, ny, nz), f32(7, 8, ny, nz)),
        [VM, VM, VM, VM, VM, VM, VM],
        (HBM, VM),
        [
            vm((7, nx + 2, rows, nz), F32),
            vm((7, nx + 2, rows, nz), F32),
            vm((4, nx, rows, nz), F32),
            vm((nx + 2, 6, rows, nz), F32),
            vm((7, nx - 8, ny, nz), F32),
            dma((1,)),
        ],
        32,
        1 << 24,
    )(active, sensitivity, velocity, omega, solid, rec_c, rec_d)

    msg_a, flux_a, st_a, fl_a = message(0, flux_b)
    pairs = [[i, i + 1] for i in range(0, lax.axis_size("gx"), 2)]
    rec_a = lax.all_gather(msg_a, "gx", axis_index_groups=pairs)

    def corrected(which, mine, theirs, st, fl, base):
        return call(
            functools.partial(respond, which),
            f32(7, nx, ny, nz),
            [VM] * 5 + [HBM],
            HBM,
            [vm((2, 7, 6, rows, nz), F32), vm((2, 6, rows, nz), F32), vm((rows, nz), F32), vm((PARTS, rows, nz), F32), vm((4, 7, ny, nz), F32), dma((4,))],
            24,
            1 << 20,
            input_output_aliases={5: 0},
        )(mine, theirs, st, fl, near, base)

    base = corrected(0, flux_a, rec_a, st_a, fl_a, base)
    return corrected(1, flux_b, rec_b, st_b, fl_b, base)


def solution(mesh):
    in_specs = (
        P(None, "gx", "gy", None),
        P(None, "gx", "gy", None),
        P("gx", "gy", None),
        P("gx", "gy", None),
        P("gx", "gy", None),
    )
    out_specs = P(None, "gx", "gy", None)
    return jax.shard_map(
        on_device, mesh=mesh, in_specs=in_specs, out_specs=out_specs, check_vma=False
    )
```

```python
import functools

import jax
import jax.numpy as jnp
from jax import lax
from jax.experimental import pallas as pl
from jax.experimental.pallas import tpu as pltpu
from jax.sharding import PartitionSpec as P

BLOCK = 16
ITERS = 4
TILE = 8
FIELDS = 11
FLUX = FIELDS
CORNER = FIELDS + 4
ROWS = CORNER + 2
PARTS = 9
SHARED = ((7, 2, 2), (0, 8, 2), (1, 4, 4), (5, 6, 4))
F32 = jnp.float32
MIB = 1 << 20

VM = pl.BlockSpec(memory_space=pltpu.VMEM)
HBM = pl.BlockSpec(memory_space=pl.ANY)


def params(mib):
    return pltpu.CompilerParams(vmem_limit_bytes=mib * MIB)


def even_index(axis):
    return lax.axis_index(axis) % 2 == 0


def lane_blocks(active, row, shape):
    lane = lax.broadcasted_iota(jnp.int32, shape, 1) // BLOCK
    out = jnp.zeros(shape, jnp.int32)
    for k in range(active.shape[1]):
        out = jnp.where(lane == k, jnp.broadcast_to(active[row:row + 1, k:k + 1], shape), out)
    return out


def rolled(v, step, axis):
    n = v.shape[axis]
    return pltpu.roll(v, (n - step) % n, axis)


def shift_z(v, step, fill):
    lane = lax.broadcasted_iota(jnp.int32, v.shape, 1)
    edge = v.shape[1] - 1 if step > 0 else 0
    return jnp.where(lane == edge, fill, rolled(v, step, 1))


def collide(h, hu, a, bc):
    s = 0.25 * h[0] + 0.125 * ((h[1] + h[2]) + (h[3] + h[4]) + (h[5] + h[6]))
    s = s + hu[0] * (h[1] - h[2]) + hu[1] * (h[3] - h[4]) + hu[2] * (h[5] - h[6])
    t = a * s
    return [t + bc * one for one in h]


def write_flags(a_ref, flags):
    a = a_ref[...]
    nf = jnp.where(a > 0.0, 0.0, 1.0).astype(F32)
    flags[0] = rolled(nf, 1, 0)
    flags[1] = rolled(nf, -1, 0)
    flags[2] = shift_z(nf, 1, 1.0)
    flags[3] = shift_z(nf, -1, 1.0)
    flags[4] = (1.0 - nf) - a
    flags[5] = nf


def advance(tiles, g, pull_1, pull_2, hu, a, flags, put, drop=False):
    if g is not None:
        g3, g4 = g[3][...], g[4][...]
        up, down = rolled(g3, 1, 0), rolled(g4, -1, 0)
    for i in range(tiles):
        r = slice(TILE * i, TILE * i + TILE)
        if g is None:
            zero = jnp.zeros((TILE, a.shape[1]), F32)
            h = [zero, pull_1(r, zero), pull_2(r, zero), zero, zero, zero, zero]
        else:
            g1, g2, g5, g6 = (g[c][r] for c in (1, 2, 5, 6))
            h = [
                g[0][r],
                pull_1(r, g2),
                pull_2(r, g1),
                up[r] + flags[0, r] * g4[r],
                down[r] + flags[1, r] * g3[r],
                shift_z(g5, 1, 0.0) + flags[2, r] * g6,
                shift_z(g6, -1, 0.0) + flags[3, r] * g5,
            ]
        if drop:
            low = lax.broadcasted_iota(jnp.int32, h[3].shape, 0) < TILE // 2
            h[3], h[4] = jnp.where(low, h[3], 0.0), jnp.where(low, 0.0, h[4])
        put(r, collide(h, [one[r] for one in hu], a[r], flags[4, r]), h)


def pack_rows(active, g, vel, omega, solid, msg_c, msg_d, gb, vb, ob, sb, ab, ping, pong, stat, fl, sem):
    is_even = even_index("gy")
    nx, ny = omega.shape[0], omega.shape[1]
    half = TILE // 2
    copies = []
    for side in range(2):
        rows, into = pl.ds((ny - half) * side, half), pl.ds(half * side, half)
        for n, (src, dst) in enumerate(((solid, sb), (omega, ob), (vel, vb), (g, gb))):
            if len(src.shape) == 4:
                window = src.at[:, :, rows, :], dst.at[:, :, into, :]
            else:
                window = src.at[:, rows, :], dst.at[:, into, :]
            copies.append(pltpu.make_async_copy(*window, sem.at[side, n]))
    copies.append(pltpu.make_async_copy(active, ab, sem.at[2, 0]))
    for copy in reversed(copies):
        copy.start()
    shape = (TILE, 128)
    zero = jnp.zeros(shape, F32)
    for x in (0, nx + 1):
        fl[x, 5] = zero
        for c in (1, 2):
            ping[c, x] = zero
            pong[c, x] = zero
    copies[-1].wait()
    low = lax.broadcasted_iota(jnp.int32, shape, 0) < half
    act = jnp.where(low, lane_blocks(ab[0], 0, shape), lane_blocks(ab[0], active.shape[1] - 1, shape))
    for copy in copies[:-1]:
        copy.wait()

    def send(k, x, below, above, row):
        first, last = below[row:row + 1], above[TILE - 1 - row:TILE - row]
        msg_c[k, x] = jnp.where(is_even, last, first)
        msg_d[k, x] = jnp.where(is_even, first, last)

    def build(x, _):
        f = ((1 - sb[x]) * act).astype(F32)
        vals = [gb[c, x] * f for c in range(7)] + [0.5 * vb[c, x] for c in range(3)] + [f * ob[x]]
        for c in range(FIELDS):
            if c < 7:
                ping[c, x + 1] = vals[c]
            else:
                stat[c - 7, x] = vals[c]
            send(c, x, vals[c], vals[c], 0)
        write_flags(stat.at[3, x], fl.at[x + 1])
        send(FLUX, x, vals[3], vals[4], 1)
        send(FLUX + 3, x, vals[10] * (0.125 - vals[8]), vals[10] * (0.125 + vals[8]), 1)
        return 0

    lax.fori_loop(0, nx, build, 0, unroll=nx)

    def step(x, t):
        old, new = (ping, pong) if t == 0 else (pong, ping)

        def pull_1(r, g2):
            return old[1, x + 2, r] + fl[x + 2, 5, r] * g2

        def pull_2(r, g1):
            return old[2, x, r] + fl[x, 5, r] * g1

        def put(r, res, h):
            if t == 0:
                for c in range(7):
                    new[c, x + 1, r] = res[c]
            send(FLUX + 1 + t, x, res[3], res[4], 1)

        gs = [old.at[c, x + 1] for c in range(7)]
        advance(1, gs, pull_1, pull_2, [stat.at[c, x] for c in range(3)], stat.at[3, x], fl.at[x + 1], put, t == 1)

    for t in range(2):

        def plane(x, _):
            step(x, t)
            return 0

        lax.fori_loop(0, nx, plane, 0, unroll=nx)

    for face in range(2):
        at = [nx - 1 if face else 0, nx - 2 if face else 1]
        for n, (p, row) in enumerate(((0, 1), (0, 2), (1, 1))):
            for c in range(4):
                plane = stat[c, at[p]]
                send(CORNER + face, 4 * n + c, plane, plane, row)
        start = gb[1 + face, at[0]] * ((1 - sb[at[0]]) * act).astype(F32)
        after = pong[1 + face, at[0] + 1]
        send(CORNER + face, 12, start, start, 1)
        send(CORNER + face, 13, after, after, 1)
        send(CORNER + face, 14, start, start, 2)
        msg_c[CORNER + face, 15] = zero[:1]
        msg_d[CORNER + face, 15] = zero[:1]


def halo_rows(rc, rd, y_even):
    def row(k, x):
        one, two = rc[k, x], rd[k, x]
        return jnp.where(y_even, one, two), jnp.where(y_even, two, one)

    return row


def placed(tile, rows, at):
    sub = lax.broadcasted_iota(jnp.int32, (TILE, 128), 0)
    return jnp.where(sub == at, rows[0], jnp.where(sub == TILE - 1 - at, rows[1], tile))


def with_flux(res, h, rows, t, x):
    sub = lax.broadcasted_iota(jnp.int32, (TILE, 128), 0)
    high, low = rows(FLUX + t, x)
    if t == 2:
        k = rows(FLUX + 3, x)
        high, low = high + k[0] * h[4], low + k[1] * h[3]
    res[3] = jnp.where(sub == 1, high, res[3])
    res[4] = jnp.where(sub == TILE - 2, low, res[4])


def all_acts(active, ny):
    nb = active.shape[1]
    return [lane_blocks(active[0], n, (ny // nb, 128)) for n in range(nb)]


def gather_plane(x, acts, g, vel, omega, solid, halo, dest, mirror):
    ny = omega.shape[1]
    half = ny // len(acts)
    f = jnp.concatenate([((1 - solid[x, n * half:(n + 1) * half]) * act).astype(F32) for n, act in enumerate(acts)], axis=0)
    for c in range(FIELDS):
        real = c
        if mirror is not None and c in (1, 2):
            real = jnp.where(mirror[0], c, 3 - c)
        own = g[real, x] * f if c < 7 else 0.5 * vel[c - 7, x] if c < 10 else f * omega[x]
        rest = halo(real)
        if mirror is not None and c == 7:
            own, rest = own * mirror[1], rest * mirror[1]
        to = dest(c)
        to[0:ny] = own
        to[ny:ny + TILE] = rest


def face(which, active, g, vel, omega, solid, rc, rd, *rest):
    msg, flux, st, fl, work = rest[-5:]
    y_even, x_even = even_index("gy"), even_index("gx")
    rc = rc.at[jnp.where(y_even, 1, 0)]
    nx, ny = omega.shape[0], omega.shape[1]
    tiles = work.shape[3] // TILE
    right = x_even if which == 0 else jnp.logical_not(x_even)
    sign = jnp.where(right, 1.0, -1.0).astype(F32)
    acts = all_acts(active, ny)
    rows = halo_rows(rc, rd, y_even)
    corner = jnp.where(right, CORNER + 1, CORNER)
    where = [jnp.where(right, nx - 1 - p, p) for p in range(4)]
    for p in range(4):

        def halo(c):
            tile = placed(jnp.zeros((TILE, 128), F32), rows(c, where[p]), 0)
            if isinstance(c, int) and c in (3, 4):
                high, low = rows(FLUX, where[p])
                sub = lax.broadcasted_iota(jnp.int32, (TILE, 128), 0)
                tile = jnp.where(sub == (1 if c == 3 else TILE - 2), high if c == 3 else low, tile)
            if isinstance(c, int) and c >= 7:
                if p == 0:
                    tile = placed(placed(tile, rows(corner, c - 7), 1), rows(corner, c - 3), 2)
                if p == 1:
                    tile = placed(tile, rows(corner, c + 1), 1)
            return tile

        gather_plane(where[p], acts, g, vel, omega, solid, halo, lambda c: work.at[0, c, p] if c < 7 else st.at[c - 7, p], (right, sign))
        write_flags(st.at[3, p], fl.at[p])
    last = slice(ny, ny + TILE)
    flux[0, 0:ny] = work[0, 2, 0, 0:ny]
    flux[0, last] = placed(placed(work[0, 2, 0, last], rows(corner, 12), 1), rows(corner, 14), 2)
    for t in range(1, 4):
        old, new = (t - 1) % 2, t % 2
        for p in range(4 - t):

            def pull_1(r, g2):
                if p == 0:
                    return jnp.zeros_like(g2)
                return work[old, 1, p - 1, r] + fl[p - 1, 5, r] * g2

            def pull_2(r, g1):
                return work[old, 2, p + 1, r] + fl[p + 1, 5, r] * g1

            def put(r, out, h):
                if t == 1 and r == last:
                    with_flux(out, h, rows, t, where[p])
                if p == 0:
                    flux[t, r] = placed(out[2], rows(corner, 13), 1) if t == 1 and r == last else out[2]
                if t < 3:
                    for c in range(7):
                        work[new, c, p, r] = out[c]

            gs = [work.at[old, c, p] for c in range(7)]
            advance(tiles, gs, pull_1, pull_2, [st.at[c, p] for c in range(3)], st.at[3, p], fl.at[p], put)

    def part(k, r):
        if k < 4:
            return flux[k, r]
        if k < 8:
            return st[0, 0, r] * sign if k == 4 else st[k - 4, 0, r]
        return st[3, 1, r] * (0.125 + st[0, 1, r])

    for k in range(PARTS):
        for i in range(ny // TILE):
            msg[k * (ny // TILE) + i] = part(k, slice(TILE * i, TILE * i + TILE))
    for n, (one, two, width) in enumerate(SHARED):
        msg[PARTS * (ny // TILE) + n] = between(part(two, last), part(one, last), width)


def between(two, one, width):
    sub = lax.broadcasted_iota(jnp.int32, (TILE, 128), 0)
    middle = (sub >= (TILE - width) // 2) & (sub < (TILE + width) // 2)
    return jnp.where(middle, pltpu.roll(two, TILE // 2, 0), one)


def unpacked(msg, parts):
    tiles = parts.shape[1] // TILE - 1
    last = slice(tiles * TILE, tiles * TILE + TILE)
    for k in range(PARTS):
        for i in range(tiles):
            parts[k, TILE * i:TILE * i + TILE] = msg[k * tiles + i]
    for n, (one, two, _) in enumerate(SHARED):
        tile = msg[PARTS * tiles + n]
        parts[one, last] = tile
        parts[two, last] = pltpu.roll(tile, TILE // 2, 0)
    parts[3, last] = jnp.zeros((TILE, 128), F32)


def interior(active, g, vel, omega, solid, rc, rd, out, near, ping, pong, stat, fl, mid, sem):
    y_even = even_index("gy")
    rc = rc.at[jnp.where(y_even, 1, 0)]
    nx, ny = omega.shape[0], omega.shape[1]
    tiles = ping.shape[2] // TILE
    acts = all_acts(active, ny)
    rows = halo_rows(rc, rd, y_even)
    for x in (0, nx + 1):
        for buf in (ping, pong):
            for c in (1, 2):
                buf[c, x] = jnp.zeros(buf.shape[2:], F32)
        fl[x, 5] = jnp.zeros(fl.shape[2:], F32)

    def build(x, _):
        def halo(c):
            tile = placed(jnp.zeros((TILE, 128), F32), rows(c, x), 0)
            sub = lax.broadcasted_iota(jnp.int32, (TILE, 128), 0)
            if c in (3, 4):
                high, low = rows(FLUX, x)
                tile = jnp.where(sub == (1 if c == 3 else TILE - 2), high if c == 3 else low, tile)
            if c == 10:
                tile = placed(tile, rows(FLUX + 3, x), 1)
            return tile

        gather_plane(x, acts, g, vel, omega, solid, halo, lambda c: ping.at[c, x + 1] if c < 7 else stat.at[c - 7, x], None)
        write_flags(stat.at[3, x], fl.at[x + 1])
        return 0

    lax.fori_loop(0, nx, build, 0, unroll=16)

    for t in range(ITERS):
        old, new = (ping, pong) if t % 2 == 0 else (pong, ping)

        def run(x, tiles, put):
            def pull_1(r, g2):
                return old[1, x + 2, r] + fl[x + 2, 5, r] * g2

            def pull_2(r, g1):
                return old[2, x, r] + fl[x, 5, r] * g1

            gs = [old.at[c, x + 1] for c in range(7)]
            advance(tiles, gs, pull_1, pull_2, [stat.at[c, x] for c in range(3)], stat.at[3, x], fl.at[x + 1], put)

        if t < ITERS - 1:

            def plane(x, _):
                def put(r, res, h):
                    if t < 2 and r.start == ny:
                        with_flux(res, h, rows, t + 1, x)
                    for c in range(7):
                        new[c, x + 1, r] = res[c]

                run(x, tiles, put)
                return 0

            lax.fori_loop(0, nx, plane, 0, unroll=16)
        else:

            def last(into, shift):
                def plane(x, _):
                    def put(r, res, h):
                        for c in range(7):
                            into[c, x - shift, r] = res[c]

                    run(x, ny // TILE, put)
                    return 0

                return plane

            lax.fori_loop(4, nx - 4, last(mid, 4), 0, unroll=4)
            store = pltpu.make_async_copy(mid, out.at[:, pl.ds(4, nx - 8)], sem.at[0])
            store.start()
            lax.fori_loop(0, 4, last(near, 0), 0, unroll=4)
            lax.fori_loop(nx - 4, nx, last(near, nx - 8), 0, unroll=4)
            store.wait()


def respond(which, mine, got, st, own, near, base, out, work, flags, hu1, theirs, done, sem):
    nx, ny = out.shape[1], out.shape[2]
    tiles = work.shape[3] // TILE
    right = even_index("gx") if which == 0 else jnp.logical_not(even_index("gx"))
    sign = jnp.where(right, 1.0, -1.0).astype(F32)
    unpacked(got.at[jnp.where(right, 1, 0)] if which == 0 else got, theirs)
    hu1[...] = theirs[4] * sign
    hu = {1: [hu1, theirs.at[5], theirs.at[6]]}
    a = {1: theirs.at[7]}
    fl = {0: flags.at[0], 1: flags.at[1]}
    for p in range(4):
        hu[2 + p] = [st.at[c, p] for c in range(3)]
        a[2 + p] = st.at[3, p]
        fl[2 + p] = own.at[p]
    write_flags(a[1], fl[1])
    fl[0][5] = jnp.where(theirs[8] > 0.0, 0.0, 1.0).astype(F32)
    live = set()
    stores = []
    for t in range(ITERS):
        old, new = t % 2, (t + 1) % 2
        todo = ((1, 2), (0, 1, 2, 3), (1, 2, 3, 4), (5, 4, 3, 2))[t]
        for q in todo:
            if q == 0:
                work[new, 1, 0] = theirs[8] * work[old, 2, 1]
                continue

            def pull_1(r, g2):
                h = fl[q - 1][5, r] * g2 if q in live else g2
                if q - 1 in live:
                    h = h + work[old, 1, q - 1, r]
                if q == 2:
                    h = h + (theirs[t, r] + fl[1][5, r] * mine[t, r])
                return h

            def pull_2(r, g1):
                h = fl[q + 1][5, r] * g1 if q in live else g1
                if q + 1 in live:
                    h = h + work[old, 2, q + 1, r]
                if q == 1:
                    h = h + (mine[t, r] + fl[2][5, r] * theirs[t, r])
                return h

            p = q - 2
            x = jnp.where(right, 7 - p, p)

            def put(r, res, h):
                if t < ITERS - 1:
                    for c in range(7):
                        work[new, c, q, r] = res[c]
                    return
                for c in range(7):
                    real = c if c not in (1, 2) else jnp.where(right, c, 3 - c)
                    done[p, real, r] = near[real, x, r] + res[c]

            if t == 0:
                for i in range(tiles):
                    r = slice(TILE * i, TILE * i + TILE)
                    k, h = (1, pull_1(r, 0.0)) if q == 2 else (2, pull_2(r, 0.0))
                    same = a[q][r] * ((0.125 + hu[q][0][r] if k == 1 else 0.125 - hu[q][0][r]) * h)
                    put(r, [same + fl[q][4, r] * h if c == k else same for c in range(7)], None)
                continue
            gs = [work.at[old, c, q] for c in range(7)] if q in live else None
            advance(tiles if t < ITERS - 1 else ny // TILE, gs, pull_1, pull_2, hu[q], a[q], fl[q], put)
            if t == ITERS - 1:
                stores.append(pltpu.make_async_copy(done.at[p], out.at[:, jnp.where(right, nx - 1 - p, p)], sem.at[p]))
                stores[-1].start()
        live = set(todo)
    for store in stores:
        store.wait()


def pair_up(x, axis, first):
    pairs = []
    for i in range(first, lax.axis_size(axis) - 1, 2):
        pairs += [(i, i + 1), (i + 1, i)]
    return lax.ppermute(x, axis, pairs)


def call(kernel, outs, ins, out_specs, scratch, mib, cost, **more):
    return pl.pallas_call(
        kernel,
        out_shape=outs,
        in_specs=ins,
        out_specs=out_specs,
        scratch_shapes=scratch,
        compiler_params=params(mib),
        cost_estimate=pl.CostEstimate(flops=cost, bytes_accessed=4 * MIB, transcendentals=0),
        **more,
    )


def on_device(sensitivity, velocity, omega, solid, active):
    nx, ny, nz = omega.shape
    rows = ny + TILE
    f32 = lambda *shape: jax.ShapeDtypeStruct(shape, F32)
    vm = pltpu.VMEM
    dma = pltpu.SemaphoreType.DMA

    pinned = [pltpu.with_memory_space_constraint(v, pltpu.HBM) for v in (active, sensitivity, velocity, omega, solid)]
    edge = lambda *shape: vm(shape + (TILE, nz), F32)
    msg_c, msg_d = call(
        pack_rows,
        (f32(ROWS, nx, 1, nz),) * 2,
        [HBM, HBM, HBM, HBM, HBM],
        (VM,) * 2,
        [edge(7, nx), edge(3, nx), edge(nx), vm((nx, TILE, nz), jnp.int32), vm(active.shape, jnp.int32), edge(7, nx + 2), edge(7, nx + 2), edge(4, nx), edge(nx + 2, 6), dma((3, 4))],
        24,
        1 << 20,
    )(*pinned)
    rec_d = pair_up(msg_d, "gy", 1)
    rec_c = lax.all_gather(msg_c, "gy", axis_index_groups=[[i, i + 1] for i in range(0, lax.axis_size("gy"), 2)])

    def message(which, *after):
        return call(
            functools.partial(face, which),
            (f32(PARTS * (ny // TILE) + len(SHARED), TILE, nz), f32(4, rows, nz), f32(4, 4, rows, nz), f32(4, 6, rows, nz)),
            [VM, VM, VM, VM, VM, VM, VM] + [HBM] * len(after),
            (VM, VM, VM, VM),
            [vm((2, 7, 4, rows, nz), F32)],
            24,
            1 << 20,
        )(active, sensitivity, velocity, omega, solid, rec_c, rec_d, *after)

    msg_b, flux_b, st_b, fl_b = message(1)
    rec_b = pair_up(msg_b, "gx", 1)
    base, near = call(
        interior,
        (f32(7, nx, ny, nz), f32(7, 8, ny, nz)),
        [VM, VM, VM, VM, VM, VM, VM],
        (HBM, VM),
        [
            vm((7, nx + 2, rows, nz), F32),
            vm((7, nx + 2, rows, nz), F32),
            vm((4, nx, rows, nz), F32),
            vm((nx + 2, 6, rows, nz), F32),
            vm((7, nx - 8, ny, nz), F32),
            dma((1,)),
        ],
        32,
        1 << 24,
    )(active, sensitivity, velocity, omega, solid, rec_c, rec_d)

    msg_a, flux_a, st_a, fl_a = message(0, flux_b)
    pairs = [[i, i + 1] for i in range(0, lax.axis_size("gx"), 2)]
    rec_a = lax.all_gather(msg_a, "gx", axis_index_groups=pairs)

    def corrected(which, mine, theirs, st, fl, base):
        return call(
            functools.partial(respond, which),
            f32(7, nx, ny, nz),
            [VM] * 5 + [HBM],
            HBM,
            [vm((2, 7, 6, rows, nz), F32), vm((2, 6, rows, nz), F32), vm((rows, nz), F32), vm((PARTS, rows, nz), F32), vm((4, 7, ny, nz), F32), dma((4,))],
            24,
            1 << 20,
            input_output_aliases={5: 0},
        )(mine, theirs, st, fl, near, base)

    base = corrected(0, flux_a, rec_a, st_a, fl_a, base)
    return corrected(1, flux_b, rec_b, st_b, fl_b, base)


def solution(mesh):
    in_specs = (
        P(None, "gx", "gy", None),
        P(None, "gx", "gy", None),
        P("gx", "gy", None),
        P("gx", "gy", None),
        P("gx", "gy", None),
    )
    out_specs = P(None, "gx", "gy", None)
    return jax.shard_map(
        on_device, mesh=mesh, in_specs=in_specs, out_specs=out_specs, check_vma=False
    )
```
